256 devices in a mesh: dp: 4 (over y_lo, core), blk: 64 (over x, z, y_hi).
Axes of the slice: x: 4, y: 4 (y_hi: 2, y_lo: 2; y = y_hi * 2 + y_lo), z: 8, core: 2. Of those that a mesh axis runs over, the one named last changes fastest.
Arguments:
- gate_pre: bfloat16 [8192, 6912], P('blk', 'dp'), may hold values from -16 to 16
- up_pre: bfloat16 [8192, 6912], P('blk', 'dp'), may hold values from -6 to 6
- down_weight: bfloat16 [6912, 2560], P(('dp', 'blk')), may hold values from -0.078125 to 0.078125
- cotangent: bfloat16 [8192, 2560], P('blk'), may hold values from -6 to 6
Outputs:
- output: bfloat16 [8192, 2560], P('blk')
- grad_weight: float32 [6912, 2560], P(('dp', 'blk'))
- grad_gate: bfloat16 [8192, 6912], P('blk', 'dp')
- grad_up: bfloat16 [8192, 6912], P('blk', 'dp')
The draws below stay inside these ranges and needn't reach their ends.
All inputs are finite; a program needn't handle non-finite values.
Results may differ from the reference program's by a relative error of at most 0.0049.
Values may be sent and summed in bfloat16 or wider, within the bound.
No kernel may reach another device: no remote copies, remote signals or barrier semaphores. Data moves between devices by JAX's collectives and lax.ppermute only.
A program may use at most 64 MiB of HBM per device.

```python
import jax
import jax.numpy as jnp

FF = 6912
DW = 2560
TOKENS = 8192


def strengthened(drawn, own_key, source, target, shards_of, factor):
    def block_of(position):
        return (jnp.arange(drawn.shape[position]) // (drawn.shape[position] // shards_of)).reshape((-1,) + (1,) * (drawn.ndim - 1 - position))

    first = jax.random.permutation(own_key, shards_of)[block_of(target)]
    other_side = (block_of(target) + shards_of // 2) % shards_of
    return jnp.where((block_of(source) == first) | (block_of(source) == other_side), factor * drawn, drawn)


def shard_levels(key, extent, pieces, least, top_value):
    factor_of, own = 1.0, jax.random.fold_in(key, 6)
    for axis_at, shards_of in pieces:
        draws = jnp.exp(jax.random.uniform(jax.random.fold_in(own, axis_at), (shards_of,), jnp.float32, least / len(pieces), top_value / len(pieces)))
        factor_of = factor_of * jnp.repeat(draws, extent[axis_at] // shards_of).reshape([-1 if axis == axis_at else 1 for axis in range(len(extent))])
    return factor_of


def centred(key, extent, deviation, bound, split=(), held_as=jnp.bfloat16):
    gain = shard_levels(key, extent, split, -0.22, 0.18) if split else 1.0
    result = jax.random.normal(key, extent, jnp.float32) * deviation * gain
    return jnp.minimum(jnp.maximum(result, -bound), bound).astype(held_as)


def heavy_noise(own_key, dims, deviation, limit, pieces, heavy, held_as=jnp.bfloat16):
    result = deviation * jax.random.normal(own_key, dims, jnp.float32)
    if pieces:
        result = result * shard_levels(own_key, dims, pieces, -0.22, 0.18)
    return jnp.clip(strengthened(result, jax.random.fold_in(own_key, 3), *heavy), -limit, limit).astype(held_as)


def setup_inputs(seed: int = 0) -> dict:
    key_list = jax.random.split(jax.random.key(seed), 5)
    return {
        "gate_pre": heavy_noise(key_list[0], (TOKENS, FF), 1.0, 16.0, ((0, 64), (1, 4)), (0, 1, 64, 4.0)),
        "up_pre": centred(key_list[1], (TOKENS, FF), 1.0, 6.0, ((0, 64), (1, 4))),
        "down_weight": centred(key_list[2], (FF, DW), FF ** -0.5, 0.078125, ((0, 256),)),
        "cotangent": centred(key_list[3], (TOKENS, DW), 1.0, 6.0, ((0, 64),)),
    }


def reference(gate_pre, up_pre, down_weight, cotangent):
    gate32 = gate_pre.astype(jnp.float32)
    up32 = up_pre.astype(jnp.float32)
    sig = jax.nn.sigmoid(gate32)
    silu_val = gate32 * sig
    hidden = (silu_val * up32).astype(jnp.bfloat16)
    output = jnp.dot(hidden, down_weight, preferred_element_type=jnp.float32).astype(jnp.bfloat16)
    back = jnp.dot(cotangent, down_weight.T, preferred_element_type=jnp.float32)
    grad_gate = (back * up32 * (sig * (1.0 + gate32 * (1.0 - sig)))).astype(jnp.bfloat16)
    grad_up = (back * silu_val).astype(jnp.bfloat16)
    scale = float(TOKENS) ** -0.5
    grad_weight = jnp.dot(hidden.T, cotangent, preferred_element_type=jnp.float32) * scale
    return output, grad_weight, grad_gate, grad_up
```

```python
import jax
import jax.numpy as jnp
from jax import lax
from jax.sharding import Mesh, PartitionSpec as P

BF16 = jnp.bfloat16
F32 = jnp.float32
NX, NZ = 4, 8


def shift(value, axis, steps):
    count = lax.axis_size(axis)
    return lax.ppermute(value, axis, [(i, (i + steps) % count) for i in range(count)])


def pick(stacked, index):
    return lax.dynamic_index_in_dim(stacked, index, 0, keepdims=False)


def swapped(value, core):
    half = value.shape[-1] // 2
    left, right = value[..., :half], value[..., half:]
    first = core == 0
    return jnp.concatenate([jnp.where(first, left, right), jnp.where(first, right, left)], -1)


def body(gate_pre, up_pre, down_weight, cotangent):
    x, z, yh, core = (lax.axis_index(a) for a in ("x", "z", "yh", "core"))
    rows, units = gate_pre.shape
    block, width = down_weight.shape
    half = width // 2
    part = units // NX

    w_mine = swapped(down_weight, core)
    w_other = shift(w_mine, "yh", 1)
    low = yh == 0
    w0 = jnp.concatenate([jnp.where(low, w_mine, w_other), jnp.where(low, w_other, w_mine)], 0)
    fwd, bwd = [w0], [w0]
    for _ in range(3):
        fwd.append(shift(fwd[-1], "z", 1))
        bwd.append(shift(bwd[-1], "z", -1))
    far = jnp.concatenate(
        [shift(fwd[3][:, :half], "z", 1), shift(bwd[3][:, half:], "z", -1)], 1
    )
    by_distance = [w0, fwd[1], fwd[2], fwd[3], far, bwd[3], bwd[2], bwd[1]]
    weight = jnp.zeros((NZ,) + w0.shape, BF16)
    for distance, piece in enumerate(by_distance):
        weight = lax.dynamic_update_index_in_dim(weight, piece, (z - distance) % NZ, 0)
    weight = weight.reshape(NZ * 2 * block, width)

    gate32, up32 = gate_pre.astype(F32), up_pre.astype(F32)
    sig = jax.nn.sigmoid(gate32)
    silu_val = gate32 * sig
    hidden = (silu_val * up32).astype(BF16)
    slices = hidden.reshape(rows, NX, part).transpose(1, 0, 2)
    cot_own = swapped(cotangent, core)
    got = []
    for k in (1, 2, 3):
        message = jnp.concatenate([cot_own[:, :half], pick(slices, (x + k) % NX)], 1)
        got.append(shift(message, "x", k))
    near = jnp.concatenate([g[:, :half] for g in got], 0)
    cot = jnp.concatenate([cot_own, jnp.concatenate([near, shift(near, "core", 1)], 1)], 0)
    hid = jnp.concatenate([pick(slices, x)] + [g[:, half:] for g in got], 0)

    scale = float(rows * NX * NZ * 2) ** (-0.5)
    grad_part = lax.dot_general(hid, cot, (((0,), (0,)), ((), ())), preferred_element_type=F32)
    grad_part = (grad_part * scale).reshape(NZ, 2 * block, width)
    farthest = pick(grad_part, (z + 4) % NZ)
    to_fwd = farthest[:, :half].astype(BF16)
    to_bwd = farthest[:, half:].astype(BF16)
    to_fwd, to_bwd = shift(to_fwd, "z", 1), shift(to_bwd, "z", -1)
    pad_fwd = jnp.pad(to_fwd.astype(F32), ((0, 0), (0, half)))
    pad_bwd = jnp.pad(to_bwd.astype(F32), ((0, 0), (half, 0)))
    to_fwd = (pick(grad_part, (z + 3) % NZ) + pad_fwd).astype(BF16)
    to_bwd = (pick(grad_part, (z - 3) % NZ) + pad_bwd).astype(BF16)
    for distance in (2, 1):
        to_fwd, to_bwd = shift(to_fwd, "z", 1), shift(to_bwd, "z", -1)
        to_fwd = (pick(grad_part, (z + distance) % NZ) + to_fwd.astype(F32)).astype(BF16)
        to_bwd = (pick(grad_part, (z - distance) % NZ) + to_bwd.astype(F32)).astype(BF16)
    to_fwd, to_bwd = shift(to_fwd, "z", 1), shift(to_bwd, "z", -1)
    grad = pick(grad_part, z) + (to_fwd.astype(F32) + to_bwd.astype(F32))
    keep = jnp.where(low, grad[:block], grad[block:])
    give = jnp.where(low, grad[block:], grad[:block]).astype(BF16)
    grad_weight = swapped(keep + shift(give, "yh", 1).astype(F32), core)

    back = lax.dot_general(cot, weight, (((1,), (1,)), ((), ())), preferred_element_type=F32)
    back = back.astype(BF16)
    out_other = jnp.dot(hid, weight[:, half:], preferred_element_type=F32).astype(BF16)
    out_mine = jnp.dot(hid, weight[:, :half], preferred_element_type=F32)
    out_mine = out_mine + shift(out_other, "core", 1).astype(F32)
    total = out_mine[:rows]
    back_own = jnp.zeros((NX, rows, part), BF16)
    back_own = lax.dynamic_update_index_in_dim(back_own, back[:rows], x, 0)
    for k in (1, 2, 3):
        here = slice(k * rows, (k + 1) * rows)
        message = jnp.concatenate([out_mine[here].astype(BF16), back[here]], 1)
        message = shift(message, "x", -k)
        total = total + message[:, :half].astype(F32)
        back_own = lax.dynamic_update_index_in_dim(back_own, message[:, half:], (x + k) % NX, 0)
    rounded = total.astype(BF16)
    out_half = (rounded.astype(F32) + shift(rounded, "yl", 1).astype(F32)).astype(BF16)
    output = swapped(jnp.concatenate([out_half, shift(out_half, "core", 1)], 1), core)

    back32 = back_own.transpose(1, 0, 2).reshape(rows, units).astype(F32)
    grad_gate = (back32 * up32 * (sig * (1.0 + gate32 * (1.0 - sig)))).astype(BF16)
    grad_up = (back32 * silu_val).astype(BF16)
    return output, grad_weight, grad_gate, grad_up


def solution(mesh):
    fine = Mesh(mesh.devices.reshape(2, 2, NX, NZ, 2), ("yl", "core", "x", "z", "yh"))
    blk, dp = ("x", "z", "yh"), ("yl", "core")
    return jax.shard_map(
        body,
        mesh=fine,
        in_specs=(P(blk, dp), P(blk, dp), P(dp + blk, None), P(blk, None)),
        out_specs=(P(blk, None), P(dp + blk, None), P(blk, dp), P(blk, dp)),
        check_vma=False,
    )
```

```python
import functools

import jax
import jax.numpy as jnp
from jax import lax
from jax.experimental import pallas as pl
from jax.experimental.pallas import tpu as pltpu
from jax.sharding import Mesh, PartitionSpec as P

BF16 = jnp.bfloat16
F32 = jnp.float32
NX, NZ = 4, 8
SLOT = 64
SENT = 56
TILE = 256


def shift(value, axis, steps):
    count = lax.axis_size(axis)
    return lax.ppermute(value, axis, [(i, (i + steps) % count) for i in range(count)])


def after(value, *others):
    return lax.optimization_barrier((value, others))[0]


def call(kernel, outs, *args, scratch=(), limit=24, flops=0, moved=None):
    whole = pl.BlockSpec(memory_space=pltpu.VMEM)
    if moved is None:
        moved = sum(a.size * a.dtype.itemsize for a in args + tuple(outs))
    return pl.pallas_call(
        kernel,
        out_shape=outs,
        in_specs=[whole] * len(args),
        out_specs=[whole] * len(outs),
        scratch_shapes=list(scratch),
        compiler_params=pltpu.CompilerParams(vmem_limit_bytes=limit * 2**20),
        cost_estimate=pl.CostEstimate(flops=flops, bytes_accessed=moved, transcendentals=0),
    )(*args)


def like(shape, dtype=BF16):
    return jax.ShapeDtypeStruct(shape, dtype)


def store_swapped(core, out, value):
    half = value.shape[1] // 2

    @pl.when(core == 0)
    def _():
        out[...] = value

    @pl.when(core != 0)
    def _():
        out[:, :half] = value[:, half:]
        out[:, half:] = value[:, :half]


def pack_weight(mine, other, out):
    rows = mine.shape[0]
    yh = lax.axis_index("yh")
    to = lax.broadcasted_iota(jnp.int32, (SENT, rows), 0)
    row = lax.broadcasted_iota(jnp.int32, (SENT, rows), 1)
    place = jnp.where(to == row + rows * yh, 1.0, 0.0).astype(BF16)
    place_other = jnp.where(to == row + rows * (1 - yh), 1.0, 0.0).astype(BF16)
    both = jnp.dot(place, mine[...], preferred_element_type=F32)
    both = both + jnp.dot(place_other, other[...], preferred_element_type=F32)
    store_swapped(lax.axis_index("core"), out, both.astype(BF16))


def prepare(gate, up, cot, m1, m2, m3, hid_own, cot_own, hidden):
    gate32, up32 = gate[...].astype(F32), up[...].astype(F32)
    units, rows = gate.shape
    half = cot.shape[1] // 2
    used = units // (NX * NZ)
    hidden[:units] = (gate32 * jax.nn.sigmoid(gate32) * up32).astype(BF16).astype(F32)
    inside = lax.broadcasted_iota(jnp.int32, (SLOT, rows), 0) < used
    padded = [
        jnp.where(inside, hidden[used * b : used * b + SLOT], 0.0).astype(BF16)
        for b in range(NX * NZ)
    ]
    for x in range(NX):

        @pl.when(lax.axis_index("x") == x)
        def _(x=x):
            for k, out in enumerate((hid_own, m1, m2, m3)):
                for block in range(NZ):
                    value = padded[(x + k) % NX * NZ + block]
                    if k == 0:
                        out[block * SLOT : (block + 1) * SLOT] = value
                    else:
                        row, column = block * SLOT % rows, half + block * SLOT // rows * rows
                        out[row : row + SLOT, column : column + rows] = value

    core = lax.axis_index("core")
    store_swapped(core, cot_own, cot[...])
    for out in (m1, m2, m3):
        out[:, :half] = cot_own[:, :half]


def stack_halves(g1, g2, g3, out):
    rows, half = g1.shape[0], out.shape[1]
    for k, got in enumerate((g1, g2, g3)):
        out[k * rows : (k + 1) * rows] = got[:, :half]


def add_up(own, h1, h2, h3, out):
    half = own.shape[1]
    total = own[...]
    for got in (h1, h2, h3):
        total = total + got[:, :half].astype(F32)
    out[...] = total.astype(BF16)


def weight_gradient(scale, cot_own, hid_own, g1, g2, g3, far, pieces, to_fwd, to_bwd, cot, hid, hid_t):
    rows, half = cot_own.shape[0], cot_own.shape[1] // 2
    cot[:rows] = cot_own[...]
    hid_t[:, :rows] = hid_own[...]
    for k, got in enumerate((g1, g2, g3)):
        here = slice((k + 1) * rows, (k + 2) * rows)
        cot[here, :half] = got[:, :half]
        cot[here, half:] = far[k * rows : (k + 1) * rows]
        for i in range(NZ * SLOT // rows):
            from_column = half + i * rows
            hid_t[i * rows : (i + 1) * rows, here] = got[:, from_column : from_column + rows]
    z = lax.axis_index("z")

    @pl.loop(0, cot.shape[1] // TILE)
    def _(t):
        columns = pl.ds(pl.multiple_of(t * TILE, TILE), TILE)
        product = jnp.dot(hid_t[...], cot[:, columns], preferred_element_type=F32) * scale
        for block in range(NZ):
            distance = lax.rem(block - z + NZ, NZ)
            pieces[distance, :, columns] = product[block * SLOT : block * SLOT + SENT]

    to_fwd[...] = pieces[4, :, :half].astype(BF16)
    to_bwd[...] = pieces[4, :, half:].astype(BF16)
    hid[...] = hid_t[...].T


def output_other(w0, f1, f2, f3, f4, b4, b3, b2, b1, hid, out, weight):
    z = lax.axis_index("z")
    half = w0.shape[1] // 2
    for distance, piece in enumerate((w0, f1, f2, f3, None, b3, b2, b1)):
        to = lax.rem(z - distance + NZ, NZ)
        if piece is None:
            weight[to, :SENT, :half] = f4[...]
            weight[to, :SENT, half:] = b4[...]
        else:
            weight[to, :SENT] = piece[...]
        weight[to, SENT:] = jnp.zeros((SLOT - SENT, w0.shape[1]), BF16)

    @pl.loop(0, half // TILE)
    def _(t):
        columns = pl.ds(pl.multiple_of(half + t * TILE, TILE), TILE)
        rhs = weight[:, :, columns].reshape(NZ * SLOT, TILE)
        product = jnp.dot(hid[...], rhs, preferred_element_type=F32)
        out[:, pl.ds(pl.multiple_of(t * TILE, TILE), TILE)] = product.astype(BF16)


def output_mine(hid, cot, weight, out, back):
    half = weight.shape[2] // 2

    @pl.loop(0, half // TILE)
    def _(t):
        columns = pl.ds(pl.multiple_of(t * TILE, TILE), TILE)
        rhs = weight[:, :, columns].reshape(NZ * SLOT, TILE)
        out[:, columns] = jnp.dot(hid[...], rhs, preferred_element_type=F32)

    slots = TILE // SLOT

    @pl.loop(0, NZ // slots)
    def _(t):
        some = weight[pl.ds(t * slots, slots)].reshape(TILE, weight.shape[2])
        product = lax.dot_general(
            some, cot[...], (((1,), (1,)), ((), ())), preferred_element_type=F32
        )
        back[pl.ds(pl.multiple_of(t * TILE, TILE), TILE)] = product.astype(BF16)


def pack_output(mine, crossed, back, total, back_own, m1, m2, m3):
    rows, half = total.shape
    total[...] = mine[:rows] + crossed[:rows].astype(F32)
    back_own[...] = back[:, :rows]
    for k, out in enumerate((m1, m2, m3)):
        here = slice((k + 1) * rows, (k + 2) * rows)
        out[:, :half] = (mine[here] + crossed[here].astype(F32)).astype(BF16)
        for i in range(NZ * SLOT // rows):
            to_column = half + i * rows
            out[:, to_column : to_column + rows] = back[i * rows : (i + 1) * rows, here]


def activation_gradients(gate, up, back_own, h1, h2, h3, grad_gate, grad_up, back32):
    units, rows = gate.shape
    half = h1.shape[1] - back_own.shape[0]
    used = units // (NX * NZ)
    for x in range(NX):

        @pl.when(lax.axis_index("x") == x)
        def _(x=x):
            for s in range(NX):
                source = (back_own, h1, h2, h3)[(s - x) % NX]
                for block in range(NZ):
                    row, column = block * SLOT, 0
                    if s != x:
                        row, column = row % rows, half + row // rows * rows
                    value = source[row : row + SLOT, column : column + rows].astype(F32)
                    start = (s * NZ + block) * used
                    back32[start : start + used] = value[:used]

    gate32, up32 = gate[...].astype(F32), up[...].astype(F32)
    sig = jax.nn.sigmoid(gate32)
    grad_gate[...] = (back32[...] * up32 * (sig * (1.0 + gate32 * (1.0 - sig)))).astype(BF16)
    grad_up[...] = (back32[...] * (gate32 * sig)).astype(BF16)


def add_pieces(distance, pieces, fwd, bwd, to_fwd, to_bwd):
    some = fwd.shape[1]
    to_fwd[:, :some] = (pieces[distance, :, :some] + fwd[...].astype(F32)).astype(BF16)
    to_bwd[:, -some:] = (pieces[NZ - distance, :, -some:] + bwd[...].astype(F32)).astype(BF16)
    if some < to_fwd.shape[1]:
        to_fwd[:, some:] = pieces[distance, :, some:].astype(BF16)
        to_bwd[:, :-some] = pieces[NZ - distance, :, :-some].astype(BF16)


def finish_rows(pieces, fwd, bwd, keep, give, total):
    rows, half = keep.shape[0], keep.shape[1] // 2
    core, yh = lax.axis_index("core"), lax.axis_index("yh")
    store_swapped(core, total, pieces[0] + (fwd[...].astype(F32) + bwd[...].astype(F32)))

    @pl.when(yh == 0)
    def _():
        keep[...] = total[:rows]
        give[...] = total[rows : 2 * rows].astype(BF16)

    @pl.when(yh != 0)
    def _():
        keep[...] = total[rows : 2 * rows]
        give[...] = total[:rows].astype(BF16)


def place_output(mine, other, out):
    half = mine.shape[1]

    @pl.when(lax.axis_index("core") == 0)
    def _():
        out[:, :half] = mine[...]
        out[:, half:] = other[...]

    @pl.when(lax.axis_index("core") != 0)
    def _():
        out[:, :half] = other[...]
        out[:, half:] = mine[...]


def body(gate_pre, up_pre, down_weight, cotangent):
    gate, up = gate_pre.T, up_pre.T
    units, rows = gate.shape
    block, width = down_weight.shape
    half = width // 2
    slots = NZ * SLOT
    tokens = NX * rows
    wide = half + slots

    w_other = shift(down_weight, "yh", 1)
    m1, m2, m3, hid_own, cot_own = call(
        prepare,
        [like((rows, wide))] * 3 + [like((slots, rows)), like((rows, width))],
        gate, up, cotangent,
        scratch=[pltpu.VMEM((units + SLOT, rows), F32)],
    )
    w_other = after(w_other, m1, m2, m3)
    (w0,) = call(pack_weight, [like((SENT, width))], down_weight, w_other)
    got = [shift(m, "x", k) for k, m in ((1, m1), (2, m2), (3, m3))]

    (near,) = call(stack_halves, [like(((NX - 1) * rows, half))], *got, flops=2 * 10**9)

    fwd, bwd = [w0], [w0]
    for step in range(3):
        f, b = shift(fwd[-1], "z", 1), shift(bwd[-1], "z", -1)
        if step == 1:
            f, b, near = lax.optimization_barrier((f, b, near))
        else:
            f, b = lax.optimization_barrier((f, b))
        fwd.append(f)
        bwd.append(b)
    far = shift(near, "core", 1)
    scale = float(tokens * NZ * 2) ** (-0.5)
    pieces, to_fwd, to_bwd, cot, hid = call(
        functools.partial(weight_gradient, scale),
        [like((NZ, SENT, width), F32)] + [like((SENT, half))] * 2 + [like((tokens, width)), like((tokens, slots))],
        cot_own, hid_own, *got, far,
        scratch=[pltpu.VMEM((slots, tokens), BF16)],
        flops=2 * slots * tokens * width,
    )

    def added(distance, ring):
        kernel = functools.partial(add_pieces, distance)
        return call(kernel, [like((SENT, width))] * 2, pieces, *ring, moved=0)

    to_fwd, to_bwd = after((to_fwd, to_bwd), fwd[3], bwd[3])
    f4, b4 = shift(fwd[3][:, :half], "z", 1), shift(bwd[3][:, half:], "z", -1)
    ring = (shift(to_fwd, "z", 1), shift(to_bwd, "z", -1))
    f4, b4, ring = lax.optimization_barrier((f4, b4, ring))
    to_fwd, to_bwd = added(3, ring)
    ring = (shift(to_fwd, "z", 1), shift(to_bwd, "z", -1))

    f4, b4 = after((f4, b4), to_fwd, to_bwd)
    out_other, weight = call(
        output_other,
        [like((tokens, half)), like((NZ, SLOT, width))],
        *fwd, f4, b4, *reversed(bwd[1:]), hid,
        flops=2 * slots * tokens * half,
    )
    crossed = shift(out_other, "core", 1)
    out_mine, back = call(
        output_mine,
        [like((tokens, half), F32), like((slots, tokens))],
        hid, cot, weight,
        flops=6 * slots * tokens * half,
    )
    crossed = after(crossed, back)
    total, back_own, m1, m2, m3 = call(
        pack_output,
        [like((rows, half), F32), like((slots, rows))] + [like((rows, wide))] * 3,
        out_mine, crossed, back,
    )
    got_back = [shift(m, "x", -k) for k, m in ((1, m1), (2, m2), (3, m3))]
    ring = after(ring, m1, m2, m3)
    to_fwd, to_bwd = added(2, ring)
    ring = lax.optimization_barrier((shift(to_fwd, "z", 1), shift(to_bwd, "z", -1)))
    to_fwd, to_bwd = added(1, ring)
    got_back = after(got_back, to_fwd, to_bwd)
    ring = (shift(to_fwd, "z", 1), shift(to_bwd, "z", -1))
    (rounded,) = call(add_up, [like((rows, half))], total, *got_back, moved=0)
    across = shift(rounded, "yl", 1)
    ring = after(ring, rounded)
    keep, give = call(
        finish_rows,
        [like((block, width), F32), like((block, width))],
        pieces, *ring,
        scratch=[pltpu.VMEM((SENT, width), F32)],
    )
    taken = shift(give, "yh", 1)
    got_back = after(got_back, give)
    grad_gate, grad_up = call(
        activation_gradients,
        [like((units, rows))] * 2,
        gate, up, back_own, *got_back,
        scratch=[pltpu.VMEM((units, rows), F32)],
        flops=15 * 10**8,
    )
    across = after(across, give)
    out_half = (rounded.astype(F32) + across.astype(F32)).astype(BF16)
    (output,) = call(place_output, [like((rows, width))], out_half, shift(out_half, "core", 1))
    grad_weight = keep + taken.astype(F32)
    return output, grad_weight, grad_gate.T, grad_up.T


def solution(mesh):
    fine = Mesh(mesh.devices.reshape(2, 2, NX, NZ, 2), ("yl", "core", "x", "z", "yh"))
    blk, dp = ("x", "z", "yh"), ("yl", "core")
    return jax.shard_map(
        body,
        mesh=fine,
        in_specs=(P(blk, dp), P(blk, dp), P(dp + blk, None), P(blk, None)),
        out_specs=(P(blk, None), P(dp + blk, None), P(blk, dp), P(blk, dp)),
        check_vma=False,
    )
```

```python
import functools

import jax
import jax.numpy as jnp
from jax import lax
from jax.experimental import pallas as pl
from jax.experimental.pallas import tpu as pltpu
from jax.sharding import Mesh, PartitionSpec as P

BF16 = jnp.bfloat16
F32 = jnp.float32
NX, NZ = 4, 8
SLOT = 64
SENT = 56
TILE = 256


def shift(value, axis, steps):
    count = lax.axis_size(axis)
    return lax.ppermute(value, axis, [(i, (i + steps) % count) for i in range(count)])


def after(value, *others):
    return lax.optimization_barrier((value, others))[0]


def call(kernel, outs, *args, scratch=(), limit=24, flops=0, moved=None):
    whole = pl.BlockSpec(memory_space=pltpu.VMEM)
    if moved is None:
        moved = sum(a.size * a.dtype.itemsize for a in args + tuple(outs))
    return pl.pallas_call(
        kernel,
        out_shape=outs,
        in_specs=[whole] * len(args),
        out_specs=[whole] * len(outs),
        scratch_shapes=list(scratch),
        compiler_params=pltpu.CompilerParams(vmem_limit_bytes=limit * 2**20),
        cost_estimate=pl.CostEstimate(flops=flops, bytes_accessed=moved, transcendentals=0),
    )(*args)


def like(shape, dtype=BF16):
    return jax.ShapeDtypeStruct(shape, dtype)


def store_swapped(core, out, value):
    half = value.shape[1] // 2

    @pl.when(core == 0)
    def _():
        out[...] = value

    @pl.when(core != 0)
    def _():
        out[:, :half] = value[:, half:]
        out[:, half:] = value[:, :half]


def pack_weight(mine, other, out):
    rows = mine.shape[0]
    yh = lax.axis_index("yh")
    to = lax.broadcasted_iota(jnp.int32, (SENT, rows), 0)
    row = lax.broadcasted_iota(jnp.int32, (SENT, rows), 1)
    place = jnp.where(to == row + rows * yh, 1.0, 0.0).astype(BF16)
    place_other = jnp.where(to == row + rows * (1 - yh), 1.0, 0.0).astype(BF16)
    both = jnp.dot(place, mine[...], preferred_element_type=F32)
    both = both + jnp.dot(place_other, other[...], preferred_element_type=F32)
    store_swapped(lax.axis_index("core"), out, both.astype(BF16))


def prepare(gate, up, cot, m1, m2, m3, hid_own, cot_own, hidden):
    gate32, up32 = gate[...].astype(F32), up[...].astype(F32)
    units, rows = gate.shape
    half = cot.shape[1] // 2
    used = units // (NX * NZ)
    hidden[:units] = (gate32 * jax.nn.sigmoid(gate32) * up32).astype(BF16).astype(F32)
    inside = lax.broadcasted_iota(jnp.int32, (SLOT, rows), 0) < used
    padded = [
        jnp.where(inside, hidden[used * b : used * b + SLOT], 0.0).astype(BF16)
        for b in range(NX * NZ)
    ]
    for x in range(NX):

        @pl.when(lax.axis_index("x") == x)
        def _(x=x):
            for k, out in enumerate((hid_own, m1, m2, m3)):
                for block in range(NZ):
                    value = padded[(x + k) % NX * NZ + block]
                    if k == 0:
                        out[block * SLOT : (block + 1) * SLOT] = value
                    else:
                        row, column = block * SLOT % rows, half + block * SLOT // rows * rows
                        out[row : row + SLOT, column : column + rows] = value

    core = lax.axis_index("core")
    store_swapped(core, cot_own, cot[...])
    for out in (m1, m2, m3):
        out[:, :half] = cot_own[:, :half]


def stack_halves(g1, g2, g3, out):
    rows, half = g1.shape[0], out.shape[1]
    for k, got in enumerate((g1, g2, g3)):
        out[k * rows : (k + 1) * rows] = got[:, :half]


def add_up(own, h1, h2, h3, out):
    total = own[...]
    for got in (h1, h2, h3):
        total = total + got[...].astype(F32)
    out[...] = total.astype(BF16)


def weight_gradient(scale, cot_own, hid_own, g1, g2, g3, far, pieces, to_bwd, cot, hid, hid_t):
    rows, half = cot_own.shape[0], cot_own.shape[1] // 2
    cot[:rows] = cot_own[...]
    hid_t[:, :rows] = hid_own[...]
    for k, got in enumerate((g1, g2, g3)):
        here = slice((k + 1) * rows, (k + 2) * rows)
        cot[here, :half] = got[:, :half]
        cot[here, half:] = far[k * rows : (k + 1) * rows]
        for i in range(NZ * SLOT // rows):
            from_column = half + i * rows
            hid_t[i * rows : (i + 1) * rows, here] = got[:, from_column : from_column + rows]
    z = lax.axis_index("z")

    @pl.loop(0, cot.shape[1] // TILE)
    def _(t):
        columns = pl.ds(pl.multiple_of(t * TILE, TILE), TILE)
        product = jnp.dot(hid_t[...], cot[:, columns], preferred_element_type=F32) * scale
        for block in range(NZ):
            distance = lax.rem(block - z + NZ, NZ)
            pieces[distance, :, columns] = product[block * SLOT : block * SLOT + SENT]

    to_bwd[...] = pieces[NZ // 2].astype(BF16)
    hid[...] = hid_t[...].T


def first_rows(value, out):
    out[...] = value[: out.shape[0], : out.shape[1]]


def output_other(w0, f1, f2, f3, f4, b3, b2, b1, hid, mark, out, weight):
    z = lax.axis_index("z")
    half = w0.shape[1] // 2
    for distance, piece in enumerate((w0, f1, f2, f3, f4, b3, b2, b1)):
        to = lax.rem(z - distance + NZ, NZ)
        weight[to, :SENT] = piece[...]
        weight[to, SENT:] = jnp.zeros((SLOT - SENT, w0.shape[1]), BF16)

    @pl.loop(0, half // TILE)
    def _(t):
        columns = pl.ds(pl.multiple_of(half + t * TILE, TILE), TILE)
        rhs = weight[:, :, columns].reshape(NZ * SLOT, TILE)
        product = jnp.dot(hid[...], rhs, preferred_element_type=F32)
        out[:, pl.ds(pl.multiple_of(t * TILE, TILE), TILE)] = product.astype(BF16)


def output_mine(hid, weight, out):
    half = weight.shape[2] // 2

    @pl.loop(0, half // TILE)
    def _(t):
        columns = pl.ds(pl.multiple_of(t * TILE, TILE), TILE)
        rhs = weight[:, :, columns].reshape(NZ * SLOT, TILE)
        out[:, columns] = jnp.dot(hid[...], rhs, preferred_element_type=F32)


def back_parts(cot, weight, *parts):
    slots = TILE // SLOT
    rows = parts[0].shape[1]

    @pl.loop(0, NZ // slots)
    def _(t):
        some = weight[pl.ds(t * slots, slots)].reshape(TILE, weight.shape[2])
        product = lax.dot_general(
            some, cot[...], (((1,), (1,)), ((), ())), preferred_element_type=F32
        )
        for k, part in enumerate(parts):
            part[pl.ds(pl.multiple_of(t * TILE, TILE), TILE)] = product[
                :, k * rows : (k + 1) * rows
            ].astype(BF16)


def pack_output(mine, crossed, total, m1, m2, m3):
    rows = total.shape[0]
    total[...] = mine[:rows] + crossed[:rows].astype(F32)
    for k, out in enumerate((m1, m2, m3)):
        here = slice((k + 1) * rows, (k + 2) * rows)
        out[...] = (mine[here] + crossed[here].astype(F32)).astype(BF16)


def activation_gradients(gate, up, b0, b1, b2, b3, grad_gate, grad_up, back32):
    units, rows = gate.shape
    used = units // (NX * NZ)
    for x in range(NX):

        @pl.when(lax.axis_index("x") == x)
        def _(x=x):
            for s in range(NX):
                source = (b0, b1, b2, b3)[(s - x) % NX]
                for block in range(NZ):
                    value = source[block * SLOT : (block + 1) * SLOT].astype(F32)
                    start = (s * NZ + block) * used
                    back32[start : start + used] = value[:used]

    gate32, up32 = gate[...].astype(F32), up[...].astype(F32)
    sig = jax.nn.sigmoid(gate32)
    grad_gate[...] = (back32[...] * up32 * (sig * (1.0 + gate32 * (1.0 - sig)))).astype(BF16)
    grad_up[...] = (back32[...] * (gate32 * sig)).astype(BF16)


def add_pieces(distance, pieces, *refs):
    *sums, to_fwd, to_bwd = refs
    here = pieces[distance]
    if len(sums) > 1:
        here = here + sums[0][...].astype(F32)
    to_fwd[...] = here.astype(BF16)
    to_bwd[...] = (pieces[NZ - distance] + sums[-1][...].astype(F32)).astype(BF16)


def finish_rows(pieces, fwd, bwd, keep, give, total):
    rows, half = keep.shape[0], keep.shape[1] // 2
    core, yh = lax.axis_index("core"), lax.axis_index("yh")
    store_swapped(core, total, pieces[0] + (fwd[...].astype(F32) + bwd[...].astype(F32)))

    @pl.when(yh == 0)
    def _():
        keep[...] = total[:rows]
        give[...] = total[rows : 2 * rows].astype(BF16)

    @pl.when(yh != 0)
    def _():
        keep[...] = total[rows : 2 * rows]
        give[...] = total[:rows].astype(BF16)


def place_output(mine, other, out):
    half = mine.shape[1]

    @pl.when(lax.axis_index("core") == 0)
    def _():
        out[:, :half] = mine[...]
        out[:, half:] = other[...]

    @pl.when(lax.axis_index("core") != 0)
    def _():
        out[:, :half] = other[...]
        out[:, half:] = mine[...]


def body(gate_pre, up_pre, down_weight, cotangent):
    gate, up = gate_pre.T, up_pre.T
    units, rows = gate.shape
    block, width = down_weight.shape
    half = width // 2
    slots = NZ * SLOT
    tokens = NX * rows
    wide = half + slots

    w_other = shift(down_weight, "yh", 1)
    m1, m2, m3, hid_own, cot_own = call(
        prepare,
        [like((rows, wide))] * 3 + [like((slots, rows)), like((rows, width))],
        gate, up, cotangent,
        scratch=[pltpu.VMEM((units + SLOT, rows), F32)],
    )
    w_other = after(w_other, m1, m2, m3)
    (w0,) = call(pack_weight, [like((SENT, width))], down_weight, w_other)
    got = [shift(m, "x", k) for k, m in ((1, m1), (2, m2), (3, m3))]

    (near,) = call(stack_halves, [like(((NX - 1) * rows, half))], *got, flops=2 * 10**9)

    fwd, bwd = [w0], [w0]
    for step in range(3):
        f, b = shift(fwd[-1], "z", 1), shift(bwd[-1], "z", -1)
        if step == 1:
            f, b, near = lax.optimization_barrier((f, b, near))
        else:
            f, b = lax.optimization_barrier((f, b))
        fwd.append(f)
        bwd.append(b)
    far = shift(near, "core", 1)
    scale = float(tokens * NZ * 2) ** (-0.5)
    pieces, to_bwd, cot, hid = call(
        functools.partial(weight_gradient, scale),
        [like((NZ, SENT, width), F32), like((SENT, width)), like((tokens, width)), like((tokens, slots))],
        cot_own, hid_own, *got, far,
        scratch=[pltpu.VMEM((slots, tokens), BF16)],
        flops=2 * slots * tokens * width,
    )

    def added(distance, ring):
        kernel = functools.partial(add_pieces, distance)
        return call(kernel, [like((SENT, width))] * 2, pieces, *ring, moved=0)

    f4 = shift(fwd[3], "z", 1)
    ring = (shift(to_bwd, "z", -1),)
    to_fwd, to_bwd = added(3, ring)
    ring = (shift(to_fwd, "z", 1), shift(to_bwd, "z", -1))

    (mark,) = call(first_rows, [like((16, 128))], to_fwd, flops=2 * 10**9)
    out_other, weight = call(
        output_other,
        [like((tokens, half)), like((NZ, SLOT, width))],
        *fwd, f4, *reversed(bwd[1:]), hid, mark,
        flops=2 * slots * tokens * half,
    )
    crossed = shift(out_other, "core", 1)
    (out_mine,) = call(
        output_mine, [like((tokens, half), F32)], hid, weight, flops=14 * 10**9
    )
    crossed = after(crossed, out_mine)
    total, m1, m2, m3 = call(
        pack_output,
        [like((rows, half), F32)] + [like((rows, half))] * 3,
        out_mine, crossed,
        flops=4 * 10**9,
    )
    got_out = [shift(m, "x", -k) for k, m in ((1, m1), (2, m2), (3, m3))]
    back_own, *backs = call(
        back_parts, [like((slots, rows))] * NX, after(cot, m1), weight, moved=0
    )
    back1, back2, back3 = backs
    got_back1, got_back3 = shift(back1, "x", -1), shift(back3, "x", -3)
    ring = after(ring, back1, back2, back3)
    to_fwd, to_bwd = added(2, ring)
    ring = lax.optimization_barrier((shift(to_fwd, "z", 1), shift(to_bwd, "z", -1)))
    to_fwd, to_bwd = added(1, ring)
    got_out = after(got_out, to_fwd, to_bwd)
    ring = (shift(to_fwd, "z", 1), shift(to_bwd, "z", -1))
    (rounded,) = call(add_up, [like((rows, half))], total, *got_out, moved=0)
    across = shift(rounded, "yl", 1)
    ring = after(ring, rounded)
    keep, give = call(
        finish_rows,
        [like((block, width), F32), like((block, width))],
        pieces, *ring,
        scratch=[pltpu.VMEM((SENT, width), F32)],
        flops=60 * 10**7,
        moved=0,
    )
    taken = shift(give, "yh", 1)
    got_back2 = shift(after(back2, give), "x", -2)
    grad_gate, grad_up = call(
        activation_gradients,
        [like((units, rows))] * 2,
        gate, up, back_own, got_back1, got_back2, got_back3,
        scratch=[pltpu.VMEM((units, rows), F32)],
        flops=60 * 10**7,
        moved=0,
    )
    across = after(across, give)
    out_half = (rounded.astype(F32) + across.astype(F32)).astype(BF16)
    (output,) = call(place_output, [like((rows, width))], out_half, shift(out_half, "core", 1))
    grad_weight = keep + taken.astype(F32)
    return output, grad_weight, grad_gate.T, grad_up.T


def solution(mesh):
    fine = Mesh(mesh.devices.reshape(2, 2, NX, NZ, 2), ("yl", "core", "x", "z", "yh"))
    blk, dp = ("x", "z", "yh"), ("yl", "core")
    return jax.shard_map(
        body,
        mesh=fine,
        in_specs=(P(blk, dp), P(blk, dp), P(dp + blk, None), P(blk, None)),
        out_specs=(P(blk, None), P(dp + blk, None), P(blk, dp), P(blk, dp)),
        check_vma=False,
    )
```

```python
import functools

import jax
import jax.numpy as jnp
from jax import lax
from jax.experimental import pallas as pl
from jax.experimental.pallas import tpu as pltpu
from jax.sharding import Mesh, PartitionSpec as P

BF16 = jnp.bfloat16
F32 = jnp.float32
NX, NZ = 4, 8
SLOT = 64
SENT = 56
TILE = 256


def shift(value, axis, steps):
    count = lax.axis_size(axis)
    return lax.ppermute(value, axis, [(i, (i + steps) % count) for i in range(count)])


def after(value, *others):
    return lax.optimization_barrier((value, others))[0]


def call(kernel, outs, *args, scratch=(), limit=24, flops=0, moved=None, space=pltpu.VMEM, out_space=pltpu.VMEM):
    if moved is None:
        moved = sum(a.size * a.dtype.itemsize for a in args + tuple(outs))
    return pl.pallas_call(
        kernel,
        out_shape=outs,
        in_specs=[pl.BlockSpec(memory_space=space)] * len(args),
        out_specs=[pl.BlockSpec(memory_space=out_space)] * len(outs),
        scratch_shapes=list(scratch),
        compiler_params=pltpu.CompilerParams(vmem_limit_bytes=limit * 2**20),
        cost_estimate=pl.CostEstimate(flops=flops, bytes_accessed=moved, transcendentals=0),
    )(*args)


def like(shape, dtype=BF16):
    return jax.ShapeDtypeStruct(shape, dtype)


def store_swapped(core, out, value):
    half = value.shape[1] // 2

    @pl.when(core == 0)
    def _():
        out[...] = value

    @pl.when(core != 0)
    def _():
        out[:, :half] = value[:, half:]
        out[:, half:] = value[:, :half]


def pack_weight(mine, other, out):
    rows = mine.shape[0]
    yh = lax.axis_index("yh")
    to = lax.broadcasted_iota(jnp.int32, (SENT, rows), 0)
    row = lax.broadcasted_iota(jnp.int32, (SENT, rows), 1)
    place = jnp.where(to == row + rows * yh, 1.0, 0.0).astype(BF16)
    place_other = jnp.where(to == row + rows * (1 - yh), 1.0, 0.0).astype(BF16)
    both = jnp.dot(place, mine[...], preferred_element_type=F32)
    both = both + jnp.dot(place_other, other[...], preferred_element_type=F32)
    store_swapped(lax.axis_index("core"), out, both.astype(BF16))


def prepare(gate_hbm, up_hbm, cot_hbm, m1, m2, m3, hid_own, cot_own, cot, gate, up, hidden, slots, sems):
    units, rows = gate.shape
    half = cot_hbm.shape[1] // 2
    part = units // NX
    used = part // NZ
    x, core = lax.axis_index("x"), lax.axis_index("core")
    started = []

    def copy(source, to):
        started.append(pltpu.make_async_copy(source, to, sems.at[len(started)]))
        started[-1].start()
        return started[-1]

    cot_loads = []
    for s in range(NX):
        here = pl.ds(s * (rows // NX), rows // NX)
        cot_loads.append(copy(cot_hbm.at[here], cot.at[here]))
    loads = []
    for s in range(NX):
        here = pl.ds(s * part, part)
        loads.append([copy(gate_hbm.at[here], gate.at[here]), copy(up_hbm.at[here], up.at[here])])
    for load in cot_loads:
        load.wait()
    mine = cot.at[:, pl.ds(pl.multiple_of(core * half, half), half)]
    other = cot.at[:, pl.ds(pl.multiple_of((1 - core) * half, half), half)]
    for out in (m1, m2, m3, cot_own):
        copy(mine, out.at[:, pl.ds(0, half)])
    copy(other, cot_own.at[:, pl.ds(half, half)])
    inside = lax.broadcasted_iota(jnp.int32, (SLOT, rows), 0) < used
    for s in range(NX):
        for load in loads[s]:
            load.wait()
        here = slice(s * part, (s + 1) * part)
        gate32, up32 = gate[here].astype(F32), up[here].astype(F32)
        hidden[here] = (gate32 * jax.nn.sigmoid(gate32) * up32).astype(BF16).astype(F32)
        for block in range(NZ):
            start = s * part + used * block
            value = jnp.where(inside, hidden[start : start + SLOT], 0.0).astype(BF16)
            row, column = block * SLOT % rows, block * SLOT // rows * rows
            slots[s, row : row + SLOT, column : column + rows] = value
    for k, out in enumerate((m1, m2, m3)):
        copy(slots.at[lax.rem(x + k + 1, NX)], out.at[:, pl.ds(half, NZ * SLOT)])
    for i in range(NZ * SLOT // rows):
        here = pl.ds(i * rows, rows)
        copy(slots.at[x, :, here], hid_own.at[here])
    for last in started[3 * NX :]:
        last.wait()


def stack_halves(g1, g2, g3, out):
    rows, half = g1.shape[0], out.shape[1]
    for k, got in enumerate((g1, g2, g3)):
        out[k * rows : (k + 1) * rows] = got[:, :half]


def add_up(own, h1, h2, h3, out):
    total = own[...]
    for got in (h1, h2, h3):
        total = total + got[...].astype(F32)
    out[...] = total.astype(BF16)


def weight_gradient(scale, cot_own, hid_own, g1, g2, g3, far, pieces, to_bwd, cot, hid, hid_t):
    rows, half = cot_own.shape[0], cot_own.shape[1] // 2
    cot[:rows] = cot_own[...]
    hid_t[:, :rows] = hid_own[...]
    for k, got in enumerate((g1, g2, g3)):
        here = slice((k + 1) * rows, (k + 2) * rows)
        cot[here, :half] = got[:, :half]
        cot[here, half:] = far[k * rows : (k + 1) * rows]
        for i in range(NZ * SLOT // rows):
            from_column = half + i * rows
            hid_t[i * rows : (i + 1) * rows, here] = got[:, from_column : from_column + rows]
    z = lax.axis_index("z")

    @pl.loop(0, cot.shape[1] // TILE)
    def _(t):
        columns = pl.ds(pl.multiple_of(t * TILE, TILE), TILE)
        product = jnp.dot(hid_t[...], cot[:, columns], preferred_element_type=F32) * scale
        for block in range(NZ):
            distance = lax.rem(block - z + NZ, NZ)
            pieces[distance, :, columns] = product[block * SLOT : block * SLOT + SENT]

    to_bwd[...] = pieces[NZ // 2].astype(BF16)
    hid[...] = hid_t[...].T


def near_blocks(w0, f1, f2, f3, b3, b2, b1, hid, weight, product, opposite, mark):
    z = lax.axis_index("z")
    width = w0.shape[1]
    for distance, piece in enumerate((w0, f1, f2, f3, None, b3, b2, b1)):
        to = lax.rem(z - distance + NZ, NZ)
        if piece is None:
            weight[to] = jnp.zeros((SLOT, width), BF16)
        else:
            weight[to, :SENT] = piece[...]
            weight[to, SENT:] = jnp.zeros((SLOT - SENT, width), BF16)

    @pl.loop(0, width // TILE)
    def _(t):
        columns = pl.ds(pl.multiple_of(t * TILE, TILE), TILE)
        rhs = weight[:, :, columns].reshape(NZ * SLOT, TILE)
        product[:, columns] = jnp.dot(hid[...], rhs, preferred_element_type=F32)

    for block in range(NZ):

        @pl.when(z == (block + NZ // 2) % NZ)
        def _(block=block):
            opposite[...] = hid[:, block * SLOT : (block + 1) * SLOT]

    mark[...] = w0[: mark.shape[0], : mark.shape[1]]


def with_opposite(first, product, opposite, block, out):
    rhs = jnp.concatenate([block[...], jnp.zeros((SLOT - SENT, block.shape[1]), BF16)], 0)
    width = out.shape[1]
    for t in range(width // TILE):
        to = slice(t * TILE, (t + 1) * TILE)
        here = slice(first + t * TILE, first + (t + 1) * TILE)
        more = jnp.dot(opposite[...], rhs[:, here], preferred_element_type=F32)
        out[:, to] = (product[:, here] + more).astype(out.dtype)


def first_rows(value, out):
    out[...] = value[: out.shape[0], : out.shape[1]]


def back_parts(cot, weight, block, *parts):
    slots = TILE // SLOT
    rows = parts[0].shape[1]
    dims = (((1,), (1,)), ((), ()))

    @pl.loop(0, NZ // slots)
    def _(t):
        some = weight[pl.ds(t * slots, slots)].reshape(TILE, weight.shape[2])
        product = lax.dot_general(some, cot[...], dims, preferred_element_type=F32)
        for k, part in enumerate(parts):
            part[pl.ds(pl.multiple_of(t * TILE, TILE), TILE)] = product[
                :, k * rows : (k + 1) * rows
            ].astype(BF16)

    opposite = lax.rem(lax.axis_index("z") + NZ // 2, NZ)
    rhs = jnp.concatenate([block[...], jnp.zeros((SLOT - SENT, block.shape[1]), BF16)], 0)
    product = lax.dot_general(rhs, cot[...], dims, preferred_element_type=F32)
    for k, part in enumerate(parts):
        part[pl.ds(pl.multiple_of(opposite * SLOT, SLOT), SLOT)] = product[
            :, k * rows : (k + 1) * rows
        ].astype(BF16)


def pack_output(mine, crossed, total, m1, m2, m3):
    rows = total.shape[0]
    total[...] = mine[:rows] + crossed[:rows].astype(F32)
    for k, out in enumerate((m1, m2, m3)):
        here = slice((k + 1) * rows, (k + 2) * rows)
        out[...] = (mine[here] + crossed[here].astype(F32)).astype(BF16)


def activation_gradients(gate, up, b0, b1, b2, b3, grad_gate, grad_up, back32):
    units, rows = gate.shape
    used = units // (NX * NZ)
    for x in range(NX):

        @pl.when(lax.axis_index("x") == x)
        def _(x=x):
            for s in range(NX):
                source = (b0, b1, b2, b3)[(s - x) % NX]
                for block in range(NZ):
                    value = source[block * SLOT : (block + 1) * SLOT].astype(F32)
                    start = (s * NZ + block) * used
                    back32[start : start + used] = value[:used]

    gate32, up32 = gate[...].astype(F32), up[...].astype(F32)
    sig = jax.nn.sigmoid(gate32)
    grad_gate[...] = (back32[...] * up32 * (sig * (1.0 + gate32 * (1.0 - sig)))).astype(BF16)
    grad_up[...] = (back32[...] * (gate32 * sig)).astype(BF16)


def add_pieces(distance, others, pieces, *refs):
    *sums, to_fwd, to_bwd = refs[others:]
    here = pieces[distance]
    if len(sums) > 1:
        here = here + sums[0][...].astype(F32)
    to_fwd[...] = here.astype(BF16)
    to_bwd[...] = (pieces[NZ - distance] + sums[-1][...].astype(F32)).astype(BF16)


def finish_rows(pieces, fwd, bwd, keep, give, total):
    rows, half = keep.shape[0], keep.shape[1] // 2
    core, yh = lax.axis_index("core"), lax.axis_index("yh")
    store_swapped(core, total, pieces[0] + (fwd[...].astype(F32) + bwd[...].astype(F32)))

    @pl.when(yh == 0)
    def _():
        keep[...] = total[:rows]
        give[...] = total[rows : 2 * rows].astype(BF16)

    @pl.when(yh != 0)
    def _():
        keep[...] = total[rows : 2 * rows]
        give[...] = total[:rows].astype(BF16)


def finish(mine, other, keep, taken, out, grad):
    half = mine.shape[1]

    @pl.when(lax.axis_index("core") == 0)
    def _():
        out[:, :half] = mine[...]
        out[:, half:] = other[...]

    @pl.when(lax.axis_index("core") != 0)
    def _():
        out[:, :half] = other[...]
        out[:, half:] = mine[...]

    grad[...] = keep[...] + taken[...].astype(F32)


def body(gate_pre, up_pre, down_weight, cotangent):
    gate, up = gate_pre.T, up_pre.T
    units, rows = gate.shape
    block, width = down_weight.shape
    half = width // 2
    slots = NZ * SLOT
    tokens = NX * rows
    wide = half + slots

    w_other = shift(down_weight, "yh", 1)
    m1, m2, m3, hid_own, cot_own = call(
        prepare,
        [like((rows, wide))] * 3 + [like((slots, rows)), like((rows, width))],
        gate, up, cotangent,
        scratch=[pltpu.VMEM((rows, width), BF16)]
        + [pltpu.VMEM((units, rows), BF16)] * 2
        + [pltpu.VMEM((units + SLOT, rows), F32), pltpu.VMEM((NX, rows, slots), BF16)]
        + [pltpu.SemaphoreType.DMA((3 * NX + 8 + slots // rows,))],
        out_space=pltpu.HBM,
        space=pltpu.HBM,
        limit=56,
    )
    w_other = after(w_other, m1, m2, m3)
    (w0,) = call(pack_weight, [like((SENT, width))], down_weight, w_other)
    got = [shift(m, "x", k) for k, m in ((1, m1), (2, m2), (3, m3))]

    (near,) = call(stack_halves, [like(((NX - 1) * rows, half))], *got, flops=2 * 10**9)

    fwd, bwd = [w0], [w0]
    for step in range(3):
        f, b = shift(fwd[-1], "z", 1), shift(bwd[-1], "z", -1)
        if step == 1:
            f, b, near = lax.optimization_barrier((f, b, near))
        else:
            f, b = lax.optimization_barrier((f, b))
        fwd.append(f)
        bwd.append(b)
    far = shift(near, "core", 1)
    scale = float(tokens * NZ * 2) ** (-0.5)
    pieces, to_bwd, cot, hid = call(
        functools.partial(weight_gradient, scale),
        [like((NZ, SENT, width), F32), like((SENT, width)), like((tokens, width)), like((tokens, slots))],
        cot_own, hid_own, *got, far,
        scratch=[pltpu.VMEM((slots, tokens), BF16)],
        flops=2 * slots * tokens * width,
    )

    def added(distance, ring, *others):
        kernel = functools.partial(add_pieces, distance, len(others))
        return call(kernel, [like((SENT, width))] * 2, pieces, *others, *ring, moved=0)

    f4 = shift(fwd[3], "z", 1)
    ring = (shift(to_bwd, "z", -1),)

    weight, product, opposite, early = call(
        near_blocks,
        [like((NZ, SLOT, width)), like((tokens, width), F32), like((tokens, SLOT)), like((16, 128))],
        *fwd, *reversed(bwd[1:]), hid,
        moved=0,
    )
    to_fwd, to_bwd = added(3, ring, early)
    ring = (shift(to_fwd, "z", 1), shift(to_bwd, "z", -1))

    (mark,) = call(first_rows, [like((16, 128))], to_fwd, flops=2 * 10**9)
    (out_other,) = call(
        lambda product, opposite, block, mark, out: with_opposite(half, product, opposite, block, out),
        [like((tokens, half))],
        product, opposite, f4, mark,
        flops=2 * slots * tokens * half,
    )
    crossed = shift(out_other, "core", 1)
    (out_mine,) = call(
        functools.partial(with_opposite, 0),
        [like((tokens, half), F32)],
        product, opposite, f4,
        flops=14 * 10**9,
    )
    crossed = after(crossed, out_mine)
    total, m1, m2, m3 = call(
        pack_output,
        [like((rows, half), F32)] + [like((rows, half))] * 3,
        out_mine, crossed,
        flops=2 * 10**9,
    )
    got_out = [shift(m, "x", -k) for k, m in ((1, m1), (2, m2), (3, m3))]
    back_own, *backs = call(
        back_parts, [like((slots, rows))] * NX, after(cot, m1), weight, f4, moved=0
    )
    back1, back2, back3 = backs
    ring = after(ring, m1, m2, m3)
    to_fwd, to_bwd = added(2, ring)
    ring = (shift(to_fwd, "z", 1), shift(to_bwd, "z", -1))
    *ring, back1, back2, back3 = lax.optimization_barrier((*ring, back1, back2, back3))
    got_back1, got_back3 = shift(back1, "x", -1), shift(back3, "x", -3)
    to_fwd, to_bwd = added(1, ring)
    got_out = after(got_out, to_fwd, to_bwd)
    ring = (shift(to_fwd, "z", 1), shift(to_bwd, "z", -1))
    (rounded,) = call(add_up, [like((rows, half))], total, *got_out, moved=0)
    across = shift(rounded, "yl", 1)
    ring = after(ring, rounded)
    keep, give = call(
        finish_rows,
        [like((block, width), F32), like((block, width))],
        pieces, *ring,
        scratch=[pltpu.VMEM((SENT, width), F32)],
        flops=60 * 10**7,
        moved=0,
    )
    taken = shift(give, "yh", 1)
    got_back2 = shift(after(back2, give), "x", -2)
    grad_gate, grad_up = call(
        activation_gradients,
        [like((units, rows))] * 2,
        gate, up, back_own, got_back1, got_back2, got_back3,
        scratch=[pltpu.VMEM((units, rows), F32)],
        flops=400 * 10**7,
        moved=0,
    )
    across = after(across, give)
    out_half = (rounded.astype(F32) + across.astype(F32)).astype(BF16)
    output, grad_weight = call(
        finish,
        [like((rows, width)), like((block, width), F32)],
        out_half, shift(out_half, "core", 1), keep, taken,
    )
    return output, grad_weight, grad_gate.T, grad_up.T


def solution(mesh):
    fine = Mesh(mesh.devices.reshape(2, 2, NX, NZ, 2), ("yl", "core", "x", "z", "yh"))
    blk, dp = ("x", "z", "yh"), ("yl", "core")
    return jax.shard_map(
        body,
        mesh=fine,
        in_specs=(P(blk, dp), P(blk, dp), P(dp + blk, None), P(blk, None)),
        out_specs=(P(blk, None), P(dp + blk, None), P(blk, dp), P(blk, dp)),
        check_vma=False,
    )
```

```python
import functools

import jax
import jax.numpy as jnp
from jax import lax
from jax.experimental import pallas as pl
from jax.experimental.pallas import tpu as pltpu
from jax.sharding import Mesh, PartitionSpec as P

BF16 = jnp.bfloat16
F32 = jnp.float32
NX, NZ = 4, 8
SLOT = 64
SENT = 56
TILE = 256


def shift(value, axis, steps):
    count = lax.axis_size(axis)
    return lax.ppermute(value, axis, [(i, (i + steps) % count) for i in range(count)])


def after(value, *others):
    return lax.optimization_barrier((value, others))[0]


def call(kernel, outs, *args, scratch=(), limit=24, flops=0, moved=None, space=pltpu.VMEM, out_space=pltpu.VMEM):
    if moved is None:
        moved = sum(a.size * a.dtype.itemsize for a in args + tuple(outs))
    return pl.pallas_call(
        kernel,
        out_shape=outs,
        in_specs=[pl.BlockSpec(memory_space=space)] * len(args),
        out_specs=[pl.BlockSpec(memory_space=out_space)] * len(outs),
        scratch_shapes=list(scratch),
        compiler_params=pltpu.CompilerParams(vmem_limit_bytes=limit * 2**20),
        cost_estimate=pl.CostEstimate(flops=flops, bytes_accessed=moved, transcendentals=0),
    )(*args)


def like(shape, dtype=BF16):
    return jax.ShapeDtypeStruct(shape, dtype)


def store_swapped(core, out, value):
    half = value.shape[1] // 2

    @pl.when(core == 0)
    def _():
        out[...] = value

    @pl.when(core != 0)
    def _():
        out[:, :half] = value[:, half:]
        out[:, half:] = value[:, :half]


def pack_weight(mine, other, out):
    rows = mine.shape[0]
    yh = lax.axis_index("yh")
    to = lax.broadcasted_iota(jnp.int32, (SENT, rows), 0)
    row = lax.broadcasted_iota(jnp.int32, (SENT, rows), 1)
    place = jnp.where(to == row + rows * yh, 1.0, 0.0).astype(BF16)
    place_other = jnp.where(to == row + rows * (1 - yh), 1.0, 0.0).astype(BF16)
    both = jnp.dot(place, mine[...], preferred_element_type=F32)
    both = both + jnp.dot(place_other, other[...], preferred_element_type=F32)
    store_swapped(lax.axis_index("core"), out, both.astype(BF16))


def prepare(gate_hbm, up_hbm, cot_hbm, m1, m2, m3, hid_own, cot_own, cot, gate, up, hidden, slots, sems):
    units, rows = gate.shape
    half = cot_hbm.shape[1] // 2
    part = units // NX
    used = part // NZ
    x, core = lax.axis_index("x"), lax.axis_index("core")
    started = []

    def copy(source, to):
        started.append(pltpu.make_async_copy(source, to, sems.at[len(started)]))
        started[-1].start()
        return started[-1]

    cot_loads = []
    for s in range(NX):
        here = pl.ds(s * (rows // NX), rows // NX)
        cot_loads.append(copy(cot_hbm.at[here], cot.at[here]))
    loads = []
    for s in range(NX):
        here = pl.ds(s * part, part)
        loads.append([copy(gate_hbm.at[here], gate.at[here]), copy(up_hbm.at[here], up.at[here])])
    for load in cot_loads:
        load.wait()
    mine = cot.at[:, pl.ds(pl.multiple_of(core * half, half), half)]
    other = cot.at[:, pl.ds(pl.multiple_of((1 - core) * half, half), half)]
    for out in (m1, m2, m3, cot_own):
        copy(mine, out.at[:, pl.ds(0, half)])
    copy(other, cot_own.at[:, pl.ds(half, half)])
    inside = lax.broadcasted_iota(jnp.int32, (SLOT, rows), 0) < used
    for s in range(NX):
        for load in loads[s]:
            load.wait()
        here = slice(s * part, (s + 1) * part)
        gate32, up32 = gate[here].astype(F32), up[here].astype(F32)
        hidden[here] = (gate32 * jax.nn.sigmoid(gate32) * up32).astype(BF16).astype(F32)
        for block in range(NZ):
            start = s * part + used * block
            value = jnp.where(inside, hidden[start : start + SLOT], 0.0).astype(BF16)
            row, column = block * SLOT % rows, block * SLOT // rows * rows
            slots[s, row : row + SLOT, column : column + rows] = value
    for k, out in enumerate((m1, m2, m3)):
        copy(slots.at[lax.rem(x + k + 1, NX)], out.at[:, pl.ds(half, NZ * SLOT)])
    for i in range(NZ * SLOT // rows):
        here = pl.ds(i * rows, rows)
        copy(slots.at[x, :, here], hid_own.at[here])
    for last in started[3 * NX :]:
        last.wait()


def stack_halves(g1, g2, g3, out):
    rows, half = g1.shape[0], out.shape[1]
    for k, got in enumerate((g1, g2, g3)):
        out[k * rows : (k + 1) * rows] = got[:, :half]


def add_up(own, h1, h2, h3, out):
    total = own[...]
    for got in (h1, h2, h3):
        total = total + got[...].astype(F32)
    out[...] = total.astype(BF16)


def weight_gradient(scale, cot_own, hid_own, g1, g2, g3, far, pieces, to_bwd, cot, hid, hid_t):
    rows, half = cot_own.shape[0], cot_own.shape[1] // 2
    cot[:rows] = cot_own[...]
    hid_t[:, :rows] = hid_own[...]
    for k, got in enumerate((g1, g2, g3)):
        here = slice((k + 1) * rows, (k + 2) * rows)
        cot[here, :half] = got[:, :half]
        cot[here, half:] = far[k * rows : (k + 1) * rows]
        for i in range(NZ * SLOT // rows):
            from_column = half + i * rows
            hid_t[i * rows : (i + 1) * rows, here] = got[:, from_column : from_column + rows]
    z = lax.axis_index("z")

    @pl.loop(0, cot.shape[1] // TILE)
    def _(t):
        columns = pl.ds(pl.multiple_of(t * TILE, TILE), TILE)
        product = jnp.dot(hid_t[...], cot[:, columns], preferred_element_type=F32) * scale
        for block in range(NZ):
            distance = lax.rem(block - z + NZ, NZ)
            pieces[distance, :, columns] = product[block * SLOT : block * SLOT + SENT]

    to_bwd[...] = pieces[NZ // 2].astype(BF16)
    hid[...] = hid_t[...].T


def padded(piece):
    rows, width = piece.shape
    return jnp.concatenate([piece[...].astype(F32), jnp.zeros((SLOT - rows, width), F32)], 0).astype(BF16)


def near_blocks(w0, f1, f2, f3, b3, b2, b1, hid, weight, product, opposite, other, mark):
    z = lax.axis_index("z")
    width = w0.shape[1]
    half = width // 2
    for distance, piece in enumerate((w0, f1, f2, f3, None, b3, b2, b1)):
        to = lax.rem(z - distance + NZ, NZ)
        if piece is None:
            weight[to] = jnp.zeros((SLOT, width), BF16)
        else:
            weight[to] = padded(piece)

    @pl.loop(0, width // TILE)
    def _(t):
        columns = pl.ds(pl.multiple_of(t * TILE, TILE), TILE)
        rhs = weight[:, :, columns].reshape(NZ * SLOT, TILE)
        product[:, columns] = jnp.dot(hid[...], rhs, preferred_element_type=F32)

    other[:, :half] = product[:, half:].astype(BF16)
    for block in range(NZ):

        @pl.when(z == (block + NZ // 2) % NZ)
        def _(block=block):
            some = hid[:, block * SLOT : (block + 1) * SLOT]
            opposite[...] = some
            other[:, half:] = jnp.concatenate([some, jnp.zeros_like(some)], 1)

    mark[...] = w0[: mark.shape[0], : mark.shape[1]]


def other_half(block, mark, out):
    out[...] = block[:, out.shape[1] :]


def output_parts(product, crossed, opposite, block, block_other, total, m1, m2, m3):
    rows, half = total.shape
    own, far = padded(block.at[:, :half]), padded(block_other)
    far_hidden = crossed[:, half : half + SLOT]
    for t in range(half // TILE):
        here = slice(t * TILE, (t + 1) * TILE)
        value = product[:, here] + crossed[:, here].astype(F32)
        value = value + jnp.dot(opposite[...], own[:, here], preferred_element_type=F32)
        value = value + jnp.dot(far_hidden, far[:, here], preferred_element_type=F32)
        total[:, here] = value[:rows]
        for k, out in enumerate((m1, m2, m3)):
            out[:, here] = value[(k + 1) * rows : (k + 2) * rows].astype(BF16)


def first_rows(value, out):
    out[...] = value[: out.shape[0], : out.shape[1]]


def back_parts(cot, weight, block, *parts):
    slots = TILE // SLOT
    rows = parts[0].shape[1]
    dims = (((1,), (1,)), ((), ()))

    @pl.loop(0, NZ // slots)
    def _(t):
        some = weight[pl.ds(t * slots, slots)].reshape(TILE, weight.shape[2])
        product = lax.dot_general(some, cot[...], dims, preferred_element_type=F32)
        for k, part in enumerate(parts):
            part[pl.ds(pl.multiple_of(t * TILE, TILE), TILE)] = product[
                :, k * rows : (k + 1) * rows
            ].astype(BF16)

    opposite = lax.rem(lax.axis_index("z") + NZ // 2, NZ)
    product = lax.dot_general(padded(block), cot[...], dims, preferred_element_type=F32)
    for k, part in enumerate(parts):
        part[pl.ds(pl.multiple_of(opposite * SLOT, SLOT), SLOT)] = product[
            :, k * rows : (k + 1) * rows
        ].astype(BF16)


def activation_gradients(gate, up, b0, b1, b2, b3, grad_gate, grad_up, back32):
    units, rows = gate.shape
    used = units // (NX * NZ)
    for x in range(NX):

        @pl.when(lax.axis_index("x") == x)
        def _(x=x):
            for s in range(NX):
                source = (b0, b1, b2, b3)[(s - x) % NX]
                for block in range(NZ):
                    value = source[block * SLOT : (block + 1) * SLOT].astype(F32)
                    start = (s * NZ + block) * used
                    back32[start : start + used] = value[:used]

    gate32, up32 = gate[...].astype(F32), up[...].astype(F32)
    sig = jax.nn.sigmoid(gate32)
    grad_gate[...] = (back32[...] * up32 * (sig * (1.0 + gate32 * (1.0 - sig)))).astype(BF16)
    grad_up[...] = (back32[...] * (gate32 * sig)).astype(BF16)


def add_pieces(distance, others, pieces, *refs):
    *sums, to_fwd, to_bwd = refs[others:]
    here = pieces[distance]
    if len(sums) > 1:
        here = here + sums[0][...].astype(F32)
    to_fwd[...] = here.astype(BF16)
    to_bwd[...] = (pieces[NZ - distance] + sums[-1][...].astype(F32)).astype(BF16)


def finish_rows(pieces, fwd, bwd, keep, give, total):
    rows, half = keep.shape[0], keep.shape[1] // 2
    core, yh = lax.axis_index("core"), lax.axis_index("yh")
    store_swapped(core, total, pieces[0] + (fwd[...].astype(F32) + bwd[...].astype(F32)))

    @pl.when(yh == 0)
    def _():
        keep[...] = total[:rows]
        give[...] = total[rows : 2 * rows].astype(BF16)

    @pl.when(yh != 0)
    def _():
        keep[...] = total[rows : 2 * rows]
        give[...] = total[:rows].astype(BF16)


def finish(mine, other, keep, taken, out, grad):
    half = mine.shape[1]

    @pl.when(lax.axis_index("core") == 0)
    def _():
        out[:, :half] = mine[...]
        out[:, half:] = other[...]

    @pl.when(lax.axis_index("core") != 0)
    def _():
        out[:, :half] = other[...]
        out[:, half:] = mine[...]

    grad[...] = keep[...] + taken[...].astype(F32)


def body(gate_pre, up_pre, down_weight, cotangent):
    gate, up = gate_pre.T, up_pre.T
    units, rows = gate.shape
    block, width = down_weight.shape
    half = width // 2
    slots = NZ * SLOT
    tokens = NX * rows
    wide = half + slots

    w_other = shift(down_weight, "yh", 1)
    m1, m2, m3, hid_own, cot_own = call(
        prepare,
        [like((rows, wide))] * 3 + [like((slots, rows)), like((rows, width))],
        gate, up, cotangent,
        scratch=[pltpu.VMEM((rows, width), BF16)]
        + [pltpu.VMEM((units, rows), BF16)] * 2
        + [pltpu.VMEM((units + SLOT, rows), F32), pltpu.VMEM((NX, rows, slots), BF16)]
        + [pltpu.SemaphoreType.DMA((3 * NX + 8 + slots // rows,))],
        out_space=pltpu.HBM,
        space=pltpu.HBM,
        limit=56,
    )
    w_other = after(w_other, m1, m2, m3)
    (w0,) = call(pack_weight, [like((SENT, width))], down_weight, w_other)
    got = [shift(m, "x", k) for k, m in ((1, m1), (2, m2), (3, m3))]

    (near,) = call(stack_halves, [like(((NX - 1) * rows, half))], *got, flops=2 * 10**9)

    fwd, bwd = [w0], [w0]
    for step in range(3):
        f, b = shift(fwd[-1], "z", 1), shift(bwd[-1], "z", -1)
        if step == 1:
            f, b, near = lax.optimization_barrier((f, b, near))
        else:
            f, b = lax.optimization_barrier((f, b))
        fwd.append(f)
        bwd.append(b)
    far = shift(near, "core", 1)
    scale = float(tokens * NZ * 2) ** (-0.5)
    pieces, to_bwd, cot, hid = call(
        functools.partial(weight_gradient, scale),
        [like((NZ, SENT, width), F32), like((SENT, width)), like((tokens, width)), like((tokens, slots))],
        cot_own, hid_own, *got, far,
        scratch=[pltpu.VMEM((slots, tokens), BF16)],
        flops=2 * slots * tokens * width,
    )

    def added(distance, ring, *others):
        kernel = functools.partial(add_pieces, distance, len(others))
        return call(kernel, [like((SENT, width))] * 2, pieces, *others, *ring, moved=0)

    f4 = shift(fwd[3], "z", 1)
    ring = (shift(to_bwd, "z", -1),)

    weight, product, opposite, other, early = call(
        near_blocks,
        [like((NZ, SLOT, width)), like((tokens, width), F32), like((tokens, SLOT))]
        + [like((tokens, half + 2 * SLOT)), like((16, 128))],
        *fwd, *reversed(bwd[1:]), hid,
        moved=0,
    )
    crossed = shift(other, "core", 1)
    to_fwd, to_bwd = added(3, ring, early)
    ring = (shift(to_fwd, "z", 1), shift(to_bwd, "z", -1))

    (mark,) = call(first_rows, [like((16, 128))], to_fwd, flops=2 * 10**9)
    (block_half,) = call(other_half, [like((SENT, half))], f4, mark, flops=14 * 10**9)
    total, m1, m2, m3 = call(
        output_parts,
        [like((rows, half), F32)] + [like((rows, half))] * 3,
        product, crossed, opposite, f4, shift(block_half, "core", 1),
        flops=1 * 10**9,
        moved=0,
    )
    got_out = [shift(m, "x", -k) for k, m in ((1, m1), (2, m2), (3, m3))]
    back_own, *backs = call(
        back_parts, [like((slots, rows))] * NX, after(cot, m1), weight, f4, moved=0
    )
    back1, back2, back3 = backs
    ring = after(ring, m1, m2, m3)
    to_fwd, to_bwd = added(2, ring)
    ring = (shift(to_fwd, "z", 1), shift(to_bwd, "z", -1))
    *ring, back1, back2, back3 = lax.optimization_barrier((*ring, back1, back2, back3))
    got_back1, got_back3 = shift(back1, "x", -1), shift(back3, "x", -3)
    to_fwd, to_bwd = added(1, ring)
    got_out = after(got_out, to_fwd, to_bwd)
    ring = (shift(to_fwd, "z", 1), shift(to_bwd, "z", -1))
    (rounded,) = call(add_up, [like((rows, half))], total, *got_out, moved=0)
    across = shift(rounded, "yl", 1)
    ring = after(ring, rounded)
    keep, give = call(
        finish_rows,
        [like((block, width), F32), like((block, width))],
        pieces, *ring,
        scratch=[pltpu.VMEM((SENT, width), F32)],
        flops=60 * 10**7,
        moved=0,
    )
    taken = shift(give, "yh", 1)
    got_back2 = shift(after(back2, give), "x", -2)
    grad_gate, grad_up = call(
        activation_gradients,
        [like((units, rows))] * 2,
        gate, up, back_own, got_back1, got_back2, got_back3,
        scratch=[pltpu.VMEM((units, rows), F32)],
        flops=400 * 10**7,
        moved=0,
    )
    across = after(across, give)
    out_half = (rounded.astype(F32) + across.astype(F32)).astype(BF16)
    output, grad_weight = call(
        finish,
        [like((rows, width)), like((block, width), F32)],
        out_half, shift(out_half, "core", 1), keep, taken,
    )
    return output, grad_weight, grad_gate.T, grad_up.T


def solution(mesh):
    fine = Mesh(mesh.devices.reshape(2, 2, NX, NZ, 2), ("yl", "core", "x", "z", "yh"))
    blk, dp = ("x", "z", "yh"), ("yl", "core")
    return jax.shard_map(
        body,
        mesh=fine,
        in_specs=(P(blk, dp), P(blk, dp), P(dp + blk, None), P(blk, None)),
        out_specs=(P(blk, None), P(dp + blk, None), P(blk, dp), P(blk, dp)),
        check_vma=False,
    )
```

```python
import functools

import jax
import jax.numpy as jnp
from jax import lax
from jax.experimental import pallas as pl
from jax.experimental.pallas import tpu as pltpu
from jax.sharding import Mesh, PartitionSpec as P

BF16 = jnp.bfloat16
F32 = jnp.float32
NX, NZ = 4, 8
SLOT = 64
SENT = 56
TILE = 256


def shift(value, axis, steps):
    count = lax.axis_size(axis)
    return lax.ppermute(value, axis, [(i, (i + steps) % count) for i in range(count)])


def after(value, *others):
    return lax.optimization_barrier((value, others))[0]


def call(kernel, outs, *args, scratch=(), limit=24, flops=0, moved=None, space=pltpu.VMEM, out_space=pltpu.VMEM):
    if moved is None:
        moved = sum(a.size * a.dtype.itemsize for a in args + tuple(outs))
    return pl.pallas_call(
        kernel,
        out_shape=outs,
        in_specs=[pl.BlockSpec(memory_space=space)] * len(args),
        out_specs=[pl.BlockSpec(memory_space=out_space)] * len(outs),
        scratch_shapes=list(scratch),
        compiler_params=pltpu.CompilerParams(vmem_limit_bytes=limit * 2**20),
        cost_estimate=pl.CostEstimate(flops=flops, bytes_accessed=moved, transcendentals=0),
    )(*args)


def like(shape, dtype=BF16):
    return jax.ShapeDtypeStruct(shape, dtype)


def store_swapped(core, out, value):
    half = value.shape[1] // 2

    @pl.when(core == 0)
    def _():
        out[...] = value

    @pl.when(core != 0)
    def _():
        out[:, :half] = value[:, half:]
        out[:, half:] = value[:, :half]


def pack_weight(mine, other, out):
    rows = mine.shape[0]
    yh = lax.axis_index("yh")
    to = lax.broadcasted_iota(jnp.int32, (SENT, rows), 0)
    row = lax.broadcasted_iota(jnp.int32, (SENT, rows), 1)
    place = jnp.where(to == row + rows * yh, 1.0, 0.0).astype(BF16)
    place_other = jnp.where(to == row + rows * (1 - yh), 1.0, 0.0).astype(BF16)
    both = jnp.dot(place, mine[...], preferred_element_type=F32)
    both = both + jnp.dot(place_other, other[...], preferred_element_type=F32)
    store_swapped(lax.axis_index("core"), out, both.astype(BF16))


def prepare(gate_hbm, up_hbm, cot_hbm, m1, m2, m3, hid_own, cot_own, cot, gate, up, hidden, slots, sems):
    units, rows = gate.shape
    half = cot_hbm.shape[1] // 2
    part = units // NX
    used = part // NZ
    x, core = lax.axis_index("x"), lax.axis_index("core")
    started = []

    def copy(source, to):
        started.append(pltpu.make_async_copy(source, to, sems.at[len(started)]))
        started[-1].start()
        return started[-1]

    cot_loads = []
    for s in range(NX):
        here = pl.ds(s * (rows // NX), rows // NX)
        cot_loads.append(copy(cot_hbm.at[here], cot.at[here]))
    loads = []
    for s in range(NX):
        here = pl.ds(s * part, part)
        loads.append([copy(gate_hbm.at[here], gate.at[here]), copy(up_hbm.at[here], up.at[here])])
    for load in cot_loads:
        load.wait()
    mine = cot.at[:, pl.ds(pl.multiple_of(core * half, half), half)]
    other = cot.at[:, pl.ds(pl.multiple_of((1 - core) * half, half), half)]
    for out in (m1, m2, m3, cot_own):
        copy(mine, out.at[:, pl.ds(0, half)])
    copy(other, cot_own.at[:, pl.ds(half, half)])
    inside = lax.broadcasted_iota(jnp.int32, (SLOT, rows), 0) < used
    for s in range(NX):
        for load in loads[s]:
            load.wait()
        here = slice(s * part, (s + 1) * part)
        gate32, up32 = gate[here].astype(F32), up[here].astype(F32)
        hidden[here] = (gate32 * jax.nn.sigmoid(gate32) * up32).astype(BF16).astype(F32)
        for block in range(NZ):
            start = s * part + used * block
            value = jnp.where(inside, hidden[start : start + SLOT], 0.0).astype(BF16)
            row, column = block * SLOT % rows, block * SLOT // rows * rows
            slots[s, row : row + SLOT, column : column + rows] = value
    for k, out in enumerate((m1, m2, m3)):
        copy(slots.at[lax.rem(x + k + 1, NX)], out.at[:, pl.ds(half, NZ * SLOT)])
    for i in range(NZ * SLOT // rows):
        here = pl.ds(i * rows, rows)
        copy(slots.at[x, :, here], hid_own.at[here])
    for last in started[3 * NX :]:
        last.wait()


def stack_halves(g1, g2, g3, out):
    rows, half = g1.shape[0], out.shape[1]
    for k, got in enumerate((g1, g2, g3)):
        out[k * rows : (k + 1) * rows] = got[:, :half]


def add_up(own, h1, h2, h3, out):
    quarter = h2.shape[1]
    low = lax.axis_index("yl") == 0
    total = own[...] + h1[...].astype(F32) + h3[...].astype(F32)
    more = h2[...].astype(F32)

    @pl.when(low)
    def _():
        out[:, :quarter] = (total[:, :quarter] + more).astype(BF16)
        out[:, quarter:] = total[:, quarter:].astype(BF16)

    @pl.when(jnp.logical_not(low))
    def _():
        out[:, :quarter] = total[:, :quarter].astype(BF16)
        out[:, quarter:] = (total[:, quarter:] + more).astype(BF16)


def weight_gradient(scale, cot_own, hid_own, g1, g2, g3, far, pieces, to_bwd, cot, hid, hid_t):
    rows, half = cot_own.shape[0], cot_own.shape[1] // 2
    cot[:rows] = cot_own[...]
    hid_t[:, :rows] = hid_own[...]
    for k, got in enumerate((g1, g2, g3)):
        here = slice((k + 1) * rows, (k + 2) * rows)
        cot[here, :half] = got[:, :half]
        cot[here, half:] = far[k * rows : (k + 1) * rows]
        for i in range(NZ * SLOT // rows):
            from_column = half + i * rows
            hid_t[i * rows : (i + 1) * rows, here] = got[:, from_column : from_column + rows]
    z = lax.axis_index("z")

    @pl.loop(0, cot.shape[1] // TILE)
    def _(t):
        columns = pl.ds(pl.multiple_of(t * TILE, TILE), TILE)
        product = jnp.dot(hid_t[...], cot[:, columns], preferred_element_type=F32) * scale
        for block in range(NZ):
            distance = lax.rem(block - z + NZ, NZ)
            pieces[distance, :, columns] = product[block * SLOT : block * SLOT + SENT]

    to_bwd[...] = pieces[NZ // 2].astype(BF16)
    hid[...] = hid_t[...].T


def padded(piece):
    rows, width = piece.shape
    return jnp.concatenate([piece[...].astype(F32), jnp.zeros((SLOT - rows, width), F32)], 0).astype(BF16)


def near_blocks(w0, f1, f2, f3, b3, b2, b1, hid, weight, product, opposite, other, mark):
    z = lax.axis_index("z")
    width = w0.shape[1]
    half = width // 2
    for distance, piece in enumerate((w0, f1, f2, f3, None, b3, b2, b1)):
        to = lax.rem(z - distance + NZ, NZ)
        if piece is None:
            weight[to] = jnp.zeros((SLOT, width), BF16)
        else:
            weight[to] = padded(piece)

    @pl.loop(0, width // TILE)
    def _(t):
        columns = pl.ds(pl.multiple_of(t * TILE, TILE), TILE)
        rhs = weight[:, :, columns].reshape(NZ * SLOT, TILE)
        product[:, columns] = jnp.dot(hid[...], rhs, preferred_element_type=F32)

    other[:, :half] = product[:, half:].astype(BF16)
    for block in range(NZ):

        @pl.when(z == (block + NZ // 2) % NZ)
        def _(block=block):
            some = hid[:, block * SLOT : (block + 1) * SLOT]
            opposite[...] = some
            other[:, half:] = jnp.concatenate([some, jnp.zeros_like(some)], 1)

    mark[...] = w0[: mark.shape[0], : mark.shape[1]]


def other_half(block, mark, out):
    out[...] = block[:, out.shape[1] :]


def output_parts(product, crossed, opposite, block, block_other, total, m1, m3, keep, give, second):
    rows, half = total.shape
    quarter = half // 2
    own, far = padded(block.at[:, :half]), padded(block_other)
    far_hidden = crossed[:, half : half + SLOT]
    for t in range(half // TILE):
        here = slice(t * TILE, (t + 1) * TILE)
        value = product[:, here] + crossed[:, here].astype(F32)
        value = value + jnp.dot(opposite[...], own[:, here], preferred_element_type=F32)
        value = value + jnp.dot(far_hidden, far[:, here], preferred_element_type=F32)
        total[:, here] = value[:rows]
        m1[:, here] = value[rows : 2 * rows].astype(BF16)
        second[:, here] = value[2 * rows : 3 * rows]
        m3[:, here] = value[3 * rows : 4 * rows].astype(BF16)

    @pl.when(lax.axis_index("yl") == 0)
    def _():
        keep[...] = second[:, :quarter]
        give[...] = second[:, quarter:].astype(BF16)

    @pl.when(lax.axis_index("yl") != 0)
    def _():
        keep[...] = second[:, quarter:]
        give[...] = second[:, :quarter].astype(BF16)


def first_rows(value, out):
    out[...] = value[: out.shape[0], : out.shape[1]]


def add_given(keep, given, out):
    out[...] = (keep[...] + given[...].astype(F32)).astype(BF16)


def back_parts(cot, weight, block, *parts):
    slots = TILE // SLOT
    rows = parts[0].shape[1]
    dims = (((1,), (1,)), ((), ()))

    @pl.loop(0, NZ // slots)
    def _(t):
        some = weight[pl.ds(t * slots, slots)].reshape(TILE, weight.shape[2])
        product = lax.dot_general(some, cot[...], dims, preferred_element_type=F32)
        for k, part in enumerate(parts):
            part[pl.ds(pl.multiple_of(t * TILE, TILE), TILE)] = product[
                :, k * rows : (k + 1) * rows
            ].astype(BF16)

    opposite = lax.rem(lax.axis_index("z") + NZ // 2, NZ)
    product = lax.dot_general(padded(block), cot[...], dims, preferred_element_type=F32)
    for k, part in enumerate(parts):
        part[pl.ds(pl.multiple_of(opposite * SLOT, SLOT), SLOT)] = product[
            :, k * rows : (k + 1) * rows
        ].astype(BF16)


def activation_gradients(gate, up, b0, b1, b2, b3, grad_gate, grad_up, back32):
    units, rows = gate.shape
    used = units // (NX * NZ)
    for x in range(NX):

        @pl.when(lax.axis_index("x") == x)
        def _(x=x):
            for s in range(NX):
                source = (b0, b1, b2, b3)[(s - x) % NX]
                for block in range(NZ):
                    value = source[block * SLOT : (block + 1) * SLOT].astype(F32)
                    start = (s * NZ + block) * used
                    back32[start : start + used] = value[:used]

    gate32, up32 = gate[...].astype(F32), up[...].astype(F32)
    sig = jax.nn.sigmoid(gate32)
    grad_gate[...] = (back32[...] * up32 * (sig * (1.0 + gate32 * (1.0 - sig)))).astype(BF16)
    grad_up[...] = (back32[...] * (gate32 * sig)).astype(BF16)


def add_pieces(distance, others, pieces, *refs):
    *sums, to_fwd, to_bwd = refs[others:]
    here = pieces[distance]
    if len(sums) > 1:
        here = here + sums[0][...].astype(F32)
    to_fwd[...] = here.astype(BF16)
    to_bwd[...] = (pieces[NZ - distance] + sums[-1][...].astype(F32)).astype(BF16)


def finish_rows(pieces, fwd, bwd, keep, give, total):
    rows, half = keep.shape[0], keep.shape[1] // 2
    core, yh = lax.axis_index("core"), lax.axis_index("yh")
    store_swapped(core, total, pieces[0] + (fwd[...].astype(F32) + bwd[...].astype(F32)))

    @pl.when(yh == 0)
    def _():
        keep[...] = total[:rows]
        give[...] = total[rows : 2 * rows].astype(BF16)

    @pl.when(yh != 0)
    def _():
        keep[...] = total[rows : 2 * rows]
        give[...] = total[:rows].astype(BF16)


def finish(mine, other, keep, taken, out, grad):
    half = mine.shape[1]

    @pl.when(lax.axis_index("core") == 0)
    def _():
        out[:, :half] = mine[...]
        out[:, half:] = other[...]

    @pl.when(lax.axis_index("core") != 0)
    def _():
        out[:, :half] = other[...]
        out[:, half:] = mine[...]

    grad[...] = keep[...] + taken[...].astype(F32)


def body(gate_pre, up_pre, down_weight, cotangent):
    gate, up = gate_pre.T, up_pre.T
    units, rows = gate.shape
    block, width = down_weight.shape
    half = width // 2
    slots = NZ * SLOT
    tokens = NX * rows
    wide = half + slots

    w_other = shift(down_weight, "yh", 1)
    m1, m2, m3, hid_own, cot_own = call(
        prepare,
        [like((rows, wide))] * 3 + [like((slots, rows)), like((rows, width))],
        gate, up, cotangent,
        scratch=[pltpu.VMEM((rows, width), BF16)]
        + [pltpu.VMEM((units, rows), BF16)] * 2
        + [pltpu.VMEM((units + SLOT, rows), F32), pltpu.VMEM((NX, rows, slots), BF16)]
        + [pltpu.SemaphoreType.DMA((3 * NX + 8 + slots // rows,))],
        out_space=pltpu.HBM,
        space=pltpu.HBM,
        limit=56,
    )
    w_other = after(w_other, m1, m2, m3)
    (w0,) = call(pack_weight, [like((SENT, width))], down_weight, w_other)
    got = [shift(m, "x", k) for k, m in ((1, m1), (2, m2), (3, m3))]

    (near,) = call(stack_halves, [like(((NX - 1) * rows, half))], *got, flops=2 * 10**9)

    fwd, bwd = [w0], [w0]
    for step in range(3):
        f, b = shift(fwd[-1], "z", 1), shift(bwd[-1], "z", -1)
        if step == 1:
            f, b, near = lax.optimization_barrier((f, b, near))
        else:
            f, b = lax.optimization_barrier((f, b))
        fwd.append(f)
        bwd.append(b)
    far = shift(near, "core", 1)
    scale = float(tokens * NZ * 2) ** (-0.5)
    pieces, to_bwd, cot, hid = call(
        functools.partial(weight_gradient, scale),
        [like((NZ, SENT, width), F32), like((SENT, width)), like((tokens, width)), like((tokens, slots))],
        cot_own, hid_own, *got, far,
        scratch=[pltpu.VMEM((slots, tokens), BF16)],
        flops=2 * slots * tokens * width,
    )

    def added(distance, ring, *others):
        kernel = functools.partial(add_pieces, distance, len(others))
        return call(kernel, [like((SENT, width))] * 2, pieces, *others, *ring, moved=0)

    f4 = shift(fwd[3], "z", 1)
    ring = (shift(to_bwd, "z", -1),)

    weight, product, opposite, other, early = call(
        near_blocks,
        [like((NZ, SLOT, width)), like((tokens, width), F32), like((tokens, SLOT))]
        + [like((tokens, half + 2 * SLOT)), like((16, 128))],
        *fwd, *reversed(bwd[1:]), hid,
        moved=0,
    )
    crossed = shift(other, "core", 1)
    to_fwd, to_bwd = added(3, ring, early)
    ring = (shift(to_fwd, "z", 1), shift(to_bwd, "z", -1))

    (mark,) = call(first_rows, [like((16, 128))], to_fwd, flops=2 * 10**9)
    (block_half,) = call(other_half, [like((SENT, half))], f4, mark, flops=14 * 10**9)
    total, m1, m3, keep2, give2 = call(
        output_parts,
        [like((rows, half), F32)] + [like((rows, half))] * 2
        + [like((rows, half // 2), F32), like((rows, half // 2))],
        product, crossed, opposite, f4, shift(block_half, "core", 1),
        scratch=[pltpu.VMEM((rows, half), F32)],
        flops=1 * 10**9,
        moved=0,
    )
    given2 = shift(give2, "yl", 1)
    got1, got3 = shift(m1, "x", -1), shift(m3, "x", -3)
    (m2,) = call(add_given, [like((rows, half // 2))], keep2, given2, moved=0)
    got_out = [got1, shift(m2, "x", -2), got3]
    back_own, *backs = call(
        back_parts, [like((slots, rows))] * NX, after(cot, m1), weight, f4, moved=0
    )
    back1, back2, back3 = backs
    ring = after(ring, m1, m3)
    to_fwd, to_bwd = added(2, ring)
    ring = (shift(to_fwd, "z", 1), shift(to_bwd, "z", -1))
    *ring, back1, back2, back3 = lax.optimization_barrier((*ring, back1, back2, back3))
    got_back1, got_back3 = shift(back1, "x", -1), shift(back3, "x", -3)
    to_fwd, to_bwd = added(1, ring)
    got_out = after(got_out, to_fwd, to_bwd)
    ring = (shift(to_fwd, "z", 1), shift(to_bwd, "z", -1))
    (rounded,) = call(add_up, [like((rows, half))], total, *got_out, moved=0)
    across = shift(rounded, "yl", 1)
    ring = after(ring, rounded)
    keep, give = call(
        finish_rows,
        [like((block, width), F32), like((block, width))],
        pieces, *ring,
        scratch=[pltpu.VMEM((SENT, width), F32)],
        flops=60 * 10**7,
        moved=0,
    )
    taken = shift(give, "yh", 1)
    got_back2 = shift(after(back2, give), "x", -2)
    grad_gate, grad_up = call(
        activation_gradients,
        [like((units, rows))] * 2,
        gate, up, back_own, got_back1, got_back2, got_back3,
        scratch=[pltpu.VMEM((units, rows), F32)],
        flops=400 * 10**7,
        moved=0,
    )
    across = after(across, give)
    out_half = (rounded.astype(F32) + across.astype(F32)).astype(BF16)
    output, grad_weight = call(
        finish,
        [like((rows, width)), like((block, width), F32)],
        out_half, shift(out_half, "core", 1), keep, taken,
    )
    return output, grad_weight, grad_gate.T, grad_up.T


def solution(mesh):
    fine = Mesh(mesh.devices.reshape(2, 2, NX, NZ, 2), ("yl", "core", "x", "z", "yh"))
    blk, dp = ("x", "z", "yh"), ("yl", "core")
    return jax.shard_map(
        body,
        mesh=fine,
        in_specs=(P(blk, dp), P(blk, dp), P(dp + blk, None), P(blk, None)),
        out_specs=(P(blk, None), P(dp + blk, None), P(blk, dp), P(blk, dp)),
        check_vma=False,
    )
```

```python
import functools

import jax
import jax.numpy as jnp
from jax import lax
from jax.experimental import pallas as pl
from jax.experimental.pallas import tpu as pltpu
from jax.sharding import Mesh, PartitionSpec as P

BF16 = jnp.bfloat16
F32 = jnp.float32
NX, NZ = 4, 8
SLOT = 64
SENT = 56
TILE = 256


def shift(value, axis, steps):
    count = lax.axis_size(axis)
    return lax.ppermute(value, axis, [(i, (i + steps) % count) for i in range(count)])


def after(value, *others):
    return lax.optimization_barrier((value, others))[0]


def call(kernel, outs, *args, scratch=(), limit=24, flops=0, moved=None, space=pltpu.VMEM, out_space=pltpu.VMEM):
    if moved is None:
        moved = sum(a.size * a.dtype.itemsize for a in args + tuple(outs))
    return pl.pallas_call(
        kernel,
        out_shape=outs,
        in_specs=[pl.BlockSpec(memory_space=space)] * len(args),
        out_specs=[pl.BlockSpec(memory_space=out_space)] * len(outs),
        scratch_shapes=list(scratch),
        compiler_params=pltpu.CompilerParams(vmem_limit_bytes=limit * 2**20),
        cost_estimate=pl.CostEstimate(flops=flops, bytes_accessed=moved, transcendentals=0),
    )(*args)


def like(shape, dtype=BF16):
    return jax.ShapeDtypeStruct(shape, dtype)


def store_swapped(core, out, value):
    half = value.shape[1] // 2

    @pl.when(core == 0)
    def _():
        out[...] = value

    @pl.when(core != 0)
    def _():
        out[:, :half] = value[:, half:]
        out[:, half:] = value[:, :half]


def pack_weight(mine, other, out):
    rows = mine.shape[0]
    yh = lax.axis_index("yh")
    to = lax.broadcasted_iota(jnp.int32, (SENT, rows), 0)
    row = lax.broadcasted_iota(jnp.int32, (SENT, rows), 1)
    place = jnp.where(to == row + rows * yh, 1.0, 0.0).astype(BF16)
    place_other = jnp.where(to == row + rows * (1 - yh), 1.0, 0.0).astype(BF16)
    both = jnp.dot(place, mine[...], preferred_element_type=F32)
    both = both + jnp.dot(place_other, other[...], preferred_element_type=F32)
    store_swapped(lax.axis_index("core"), out, both.astype(BF16))


def prepare(gate_hbm, up_hbm, cot_hbm, m1, m2, m3, hid_own, cot_own, cot, gate, up, hidden, slots, sems):
    units, rows = gate.shape
    half = cot_hbm.shape[1] // 2
    part = units // NX
    used = part // NZ
    x, core = lax.axis_index("x"), lax.axis_index("core")
    started = []

    def copy(source, to):
        started.append(pltpu.make_async_copy(source, to, sems.at[len(started)]))
        started[-1].start()
        return started[-1]

    cot_loads = []
    for s in range(NX):
        here = pl.ds(s * (rows // NX), rows // NX)
        cot_loads.append(copy(cot_hbm.at[here], cot.at[here]))
    loads = []
    for s in range(NX):
        here = pl.ds(s * part, part)
        loads.append([copy(gate_hbm.at[here], gate.at[here]), copy(up_hbm.at[here], up.at[here])])
    for load in cot_loads:
        load.wait()
    mine = cot.at[:, pl.ds(pl.multiple_of(core * half, half), half)]
    other = cot.at[:, pl.ds(pl.multiple_of((1 - core) * half, half), half)]
    for out in (m1, m3, cot_own):
        copy(mine, out.at[:, pl.ds(0, half)])
    quarter = half // 2
    start = pl.multiple_of(core * half + lax.axis_index("yl") * quarter, quarter)
    copy(cot.at[:, pl.ds(start, quarter)], m2.at[:, pl.ds(0, quarter)])
    copy(other, cot_own.at[:, pl.ds(half, half)])
    inside = lax.broadcasted_iota(jnp.int32, (SLOT, rows), 0) < used
    for s in range(NX):
        for load in loads[s]:
            load.wait()
        here = slice(s * part, (s + 1) * part)
        gate32, up32 = gate[here].astype(F32), up[here].astype(F32)
        hidden[here] = (gate32 * jax.nn.sigmoid(gate32) * up32).astype(BF16).astype(F32)
        for block in range(NZ):
            start = s * part + used * block
            value = jnp.where(inside, hidden[start : start + SLOT], 0.0).astype(BF16)
            row, column = block * SLOT % rows, block * SLOT // rows * rows
            slots[s, row : row + SLOT, column : column + rows] = value
    for k, out in enumerate((m1, m2, m3)):
        start = out.shape[1] - NZ * SLOT
        copy(slots.at[lax.rem(x + k + 1, NX)], out.at[:, pl.ds(start, NZ * SLOT)])
    for i in range(NZ * SLOT // rows):
        here = pl.ds(i * rows, rows)
        copy(slots.at[x, :, here], hid_own.at[here])
    for last in started[3 * NX :]:
        last.wait()


def near_halves(g1, g2, g3, swapped2, n1, n2, n3):
    half = n1.shape[1]
    quarter = half // 2
    n1[...] = g1[:, :half]
    n3[...] = g3[:, :half]

    @pl.when(lax.axis_index("yl") == 0)
    def _():
        n2[:, :quarter] = g2[:, :quarter]
        n2[:, quarter:] = swapped2[:, :quarter]

    @pl.when(lax.axis_index("yl") != 0)
    def _():
        n2[:, :quarter] = swapped2[:, :quarter]
        n2[:, quarter:] = g2[:, :quarter]


def add_up(own, h1, h2, h3, out):
    quarter = h2.shape[1]
    low = lax.axis_index("yl") == 0
    total = own[...] + h1[...].astype(F32) + h3[...].astype(F32)
    more = h2[...].astype(F32)

    @pl.when(low)
    def _():
        out[:, :quarter] = (total[:, :quarter] + more).astype(BF16)
        out[:, quarter:] = total[:, quarter:].astype(BF16)

    @pl.when(jnp.logical_not(low))
    def _():
        out[:, :quarter] = total[:, :quarter].astype(BF16)
        out[:, quarter:] = (total[:, quarter:] + more).astype(BF16)


def weight_gradient(scale, cot_own, hid_own, g1, g2, g3, n2, f1, f2, f3, pieces, to_bwd, cot, hid, hid_t):
    rows, half = cot_own.shape[0], cot_own.shape[1] // 2
    cot[:rows] = cot_own[...]
    hid_t[:, :rows] = hid_own[...]
    for k, (got, near, far) in enumerate(((g1, g1, f1), (g2, n2, f2), (g3, g3, f3))):
        here = slice((k + 1) * rows, (k + 2) * rows)
        cot[here, :half] = near[:, :half]
        cot[here, half:] = far[...]
        for i in range(NZ * SLOT // rows):
            from_column = got.shape[1] - NZ * SLOT + i * rows
            hid_t[i * rows : (i + 1) * rows, here] = got[:, from_column : from_column + rows]
    z = lax.axis_index("z")

    @pl.loop(0, cot.shape[1] // TILE)
    def _(t):
        columns = pl.ds(pl.multiple_of(t * TILE, TILE), TILE)
        product = jnp.dot(hid_t[...], cot[:, columns], preferred_element_type=F32) * scale
        for block in range(NZ):
            distance = lax.rem(block - z + NZ, NZ)
            pieces[distance, :, columns] = product[block * SLOT : block * SLOT + SENT]

    to_bwd[...] = pieces[NZ // 2].astype(BF16)
    hid[...] = hid_t[...].T


def padded(piece):
    rows, width = piece.shape
    return jnp.concatenate([piece[...].astype(F32), jnp.zeros((SLOT - rows, width), F32)], 0).astype(BF16)


def near_blocks(w0, f1, f2, f3, b3, b2, b1, hid, weight, product, opposite, other, mark):
    z = lax.axis_index("z")
    width = w0.shape[1]
    half = width // 2
    for distance, piece in enumerate((w0, f1, f2, f3, None, b3, b2, b1)):
        to = lax.rem(z - distance + NZ, NZ)
        if piece is None:
            weight[to] = jnp.zeros((SLOT, width), BF16)
        else:
            weight[to] = padded(piece)

    @pl.loop(0, width // TILE)
    def _(t):
        columns = pl.ds(pl.multiple_of(t * TILE, TILE), TILE)
        rhs = weight[:, :, columns].reshape(NZ * SLOT, TILE)
        product[:, columns] = jnp.dot(hid[...], rhs, preferred_element_type=F32)

    other[:, :half] = product[:, half:].astype(BF16)
    for block in range(NZ):

        @pl.when(z == (block + NZ // 2) % NZ)
        def _(block=block):
            some = hid[:, block * SLOT : (block + 1) * SLOT]
            opposite[...] = some
            other[:, half:] = jnp.concatenate([some, jnp.zeros_like(some)], 1)

    mark[...] = w0[: mark.shape[0], : mark.shape[1]]


def other_half(block, mark, out):
    out[...] = block[:, out.shape[1] :]


def output_parts(product, crossed, opposite, block, block_other, total, m1, m3, keep, give, second):
    rows, half = total.shape
    quarter = half // 2
    own, far = padded(block.at[:, :half]), padded(block_other)
    far_hidden = crossed[:, half : half + SLOT]
    for t in range(half // TILE):
        here = slice(t * TILE, (t + 1) * TILE)
        value = product[:, here] + crossed[:, here].astype(F32)
        value = value + jnp.dot(opposite[...], own[:, here], preferred_element_type=F32)
        value = value + jnp.dot(far_hidden, far[:, here], preferred_element_type=F32)
        total[:, here] = value[:rows]
        m1[:, here] = value[rows : 2 * rows].astype(BF16)
        second[:, here] = value[2 * rows : 3 * rows]
        m3[:, here] = value[3 * rows : 4 * rows].astype(BF16)

    @pl.when(lax.axis_index("yl") == 0)
    def _():
        keep[...] = second[:, :quarter]
        give[...] = second[:, quarter:].astype(BF16)

    @pl.when(lax.axis_index("yl") != 0)
    def _():
        keep[...] = second[:, quarter:]
        give[...] = second[:, :quarter].astype(BF16)


def first_rows(value, out):
    out[...] = value[: out.shape[0], : out.shape[1]]


def add_given(keep, given, out):
    out[...] = (keep[...] + given[...].astype(F32)).astype(BF16)


def back_parts(cot, weight, block, *parts):
    slots = TILE // SLOT
    rows = parts[0].shape[1]
    dims = (((1,), (1,)), ((), ()))

    @pl.loop(0, NZ // slots)
    def _(t):
        some = weight[pl.ds(t * slots, slots)].reshape(TILE, weight.shape[2])
        product = lax.dot_general(some, cot[...], dims, preferred_element_type=F32)
        for k, part in enumerate(parts):
            part[pl.ds(pl.multiple_of(t * TILE, TILE), TILE)] = product[
                :, k * rows : (k + 1) * rows
            ].astype(BF16)

    opposite = lax.rem(lax.axis_index("z") + NZ // 2, NZ)
    product = lax.dot_general(padded(block), cot[...], dims, preferred_element_type=F32)
    for k, part in enumerate(parts):
        part[pl.ds(pl.multiple_of(opposite * SLOT, SLOT), SLOT)] = product[
            :, k * rows : (k + 1) * rows
        ].astype(BF16)


def activation_gradients(gate, up, b0, b1, b2, b3, grad_gate, grad_up, back32):
    units, rows = gate.shape
    used = units // (NX * NZ)
    for x in range(NX):

        @pl.when(lax.axis_index("x") == x)
        def _(x=x):
            for s in range(NX):
                source = (b0, b1, b2, b3)[(s - x) % NX]
                for block in range(NZ):
                    value = source[block * SLOT : (block + 1) * SLOT].astype(F32)
                    start = (s * NZ + block) * used
                    back32[start : start + used] = value[:used]

    gate32, up32 = gate[...].astype(F32), up[...].astype(F32)
    sig = jax.nn.sigmoid(gate32)
    grad_gate[...] = (back32[...] * up32 * (sig * (1.0 + gate32 * (1.0 - sig)))).astype(BF16)
    grad_up[...] = (back32[...] * (gate32 * sig)).astype(BF16)


def add_pieces(distance, others, pieces, *refs):
    *sums, to_fwd, to_bwd = refs[others:]
    here = pieces[distance]
    if len(sums) > 1:
        here = here + sums[0][...].astype(F32)
    to_fwd[...] = here.astype(BF16)
    to_bwd[...] = (pieces[NZ - distance] + sums[-1][...].astype(F32)).astype(BF16)


def finish_rows(pieces, fwd, bwd, keep, give, total):
    rows, half = keep.shape[0], keep.shape[1] // 2
    core, yh = lax.axis_index("core"), lax.axis_index("yh")
    store_swapped(core, total, pieces[0] + (fwd[...].astype(F32) + bwd[...].astype(F32)))

    @pl.when(yh == 0)
    def _():
        keep[...] = total[:rows]
        give[...] = total[rows : 2 * rows].astype(BF16)

    @pl.when(yh != 0)
    def _():
        keep[...] = total[rows : 2 * rows]
        give[...] = total[:rows].astype(BF16)


def finish(mine, other, keep, taken, out, grad):
    half = mine.shape[1]

    @pl.when(lax.axis_index("core") == 0)
    def _():
        out[:, :half] = mine[...]
        out[:, half:] = other[...]

    @pl.when(lax.axis_index("core") != 0)
    def _():
        out[:, :half] = other[...]
        out[:, half:] = mine[...]

    grad[...] = keep[...] + taken[...].astype(F32)


def body(gate_pre, up_pre, down_weight, cotangent):
    gate, up = gate_pre.T, up_pre.T
    units, rows = gate.shape
    block, width = down_weight.shape
    half = width // 2
    slots = NZ * SLOT
    tokens = NX * rows
    wide = half + slots

    w_other = shift(down_weight, "yh", 1)
    m1, m2, m3, hid_own, cot_own = call(
        prepare,
        [like((rows, wide)), like((rows, wide - half // 2)), like((rows, wide))]
        + [like((slots, rows)), like((rows, width))],
        gate, up, cotangent,
        scratch=[pltpu.VMEM((rows, width), BF16)]
        + [pltpu.VMEM((units, rows), BF16)] * 2
        + [pltpu.VMEM((units + SLOT, rows), F32), pltpu.VMEM((NX, rows, slots), BF16)]
        + [pltpu.SemaphoreType.DMA((3 * NX + 8 + slots // rows,))],
        out_space=pltpu.HBM,
        space=pltpu.HBM,
        limit=56,
    )
    w_other = after(w_other, m1, m2, m3)
    (w0,) = call(pack_weight, [like((SENT, width))], down_weight, w_other, flops=18 * 10**8)
    got = [shift(m, "x", k) for k, m in ((1, m1), (2, m2), (3, m3))]

    nears = call(
        near_halves,
        [like((rows, half))] * 3,
        *got, shift(got[1], "yl", 1),
        flops=200 * 10**6,
        moved=0,
    )
    far = [shift(near, "core", 1) for near in nears]

    fwd, bwd = [w0], [w0]
    for step in range(3):
        f, b = shift(fwd[-1], "z", 1), shift(bwd[-1], "z", -1)
        f, b = lax.optimization_barrier((f, b))
        fwd.append(f)
        bwd.append(b)
    scale = float(tokens * NZ * 2) ** (-0.5)
    pieces, to_bwd, cot, hid = call(
        functools.partial(weight_gradient, scale),
        [like((NZ, SENT, width), F32), like((SENT, width)), like((tokens, width)), like((tokens, slots))],
        cot_own, hid_own, *got, nears[1], *far,
        scratch=[pltpu.VMEM((slots, tokens), BF16)],
        flops=0,
        moved=0,
    )

    def added(distance, ring, *others):
        kernel = functools.partial(add_pieces, distance, len(others))
        return call(kernel, [like((SENT, width))] * 2, pieces, *others, *ring, moved=0)

    fwd[3], to_bwd = lax.optimization_barrier((fwd[3], to_bwd))
    f4 = shift(fwd[3], "z", 1)
    ring = (shift(to_bwd, "z", -1),)

    weight, product, opposite, other, early = call(
        near_blocks,
        [like((NZ, SLOT, width)), like((tokens, width), F32), like((tokens, SLOT))]
        + [like((tokens, half + 2 * SLOT)), like((16, 128))],
        *fwd, *reversed(bwd[1:]), hid,
        moved=0,
    )
    crossed = shift(other, "core", 1)
    to_fwd, to_bwd = added(3, ring, early)
    ring = (shift(to_fwd, "z", 1), shift(to_bwd, "z", -1))

    (mark,) = call(first_rows, [like((16, 128))], to_fwd, flops=2 * 10**9)
    (block_half,) = call(other_half, [like((SENT, half))], f4, mark, flops=14 * 10**9)
    total, m1, m3, keep2, give2 = call(
        output_parts,
        [like((rows, half), F32)] + [like((rows, half))] * 2
        + [like((rows, half // 2), F32), like((rows, half // 2))],
        product, crossed, opposite, f4, shift(block_half, "core", 1),
        scratch=[pltpu.VMEM((rows, half), F32)],
        flops=1 * 10**9,
        moved=0,
    )
    given2 = shift(give2, "yl", 1)
    got1, got3 = shift(m1, "x", -1), shift(m3, "x", -3)
    (m2,) = call(add_given, [like((rows, half // 2))], keep2, given2, moved=0)
    got_out = [got1, shift(m2, "x", -2), got3]
    back_own, *backs = call(
        back_parts, [like((slots, rows))] * NX, after(cot, m1), weight, f4, moved=0
    )
    back1, back2, back3 = backs
    ring = after(ring, m1, m3)
    to_fwd, to_bwd = added(2, ring)
    ring = (shift(to_fwd, "z", 1), shift(to_bwd, "z", -1))
    *ring, back1, back2, back3 = lax.optimization_barrier((*ring, back1, back2, back3))
    got_back1, got_back3 = shift(back1, "x", -1), shift(back3, "x", -3)
    to_fwd, to_bwd = added(1, ring)
    got_out = after(got_out, to_fwd, to_bwd)
    ring = (shift(to_fwd, "z", 1), shift(to_bwd, "z", -1))
    (rounded,) = call(add_up, [like((rows, half))], total, *got_out, moved=0)
    across = shift(rounded, "yl", 1)
    ring = after(ring, rounded)
    keep, give = call(
        finish_rows,
        [like((block, width), F32), like((block, width))],
        pieces, *ring,
        scratch=[pltpu.VMEM((SENT, width), F32)],
        flops=60 * 10**7,
        moved=0,
    )
    taken = shift(give, "yh", 1)
    got_back2 = shift(after(back2, give), "x", -2)
    grad_gate, grad_up = call(
        activation_gradients,
        [like((units, rows))] * 2,
        gate, up, back_own, got_back1, got_back2, got_back3,
        scratch=[pltpu.VMEM((units, rows), F32)],
        flops=400 * 10**7,
        moved=0,
    )
    across = after(across, give)
    out_half = (rounded.astype(F32) + across.astype(F32)).astype(BF16)
    output, grad_weight = call(
        finish,
        [like((rows, width)), like((block, width), F32)],
        out_half, shift(out_half, "core", 1), keep, taken,
    )
    return output, grad_weight, grad_gate.T, grad_up.T


def solution(mesh):
    fine = Mesh(mesh.devices.reshape(2, 2, NX, NZ, 2), ("yl", "core", "x", "z", "yh"))
    blk, dp = ("x", "z", "yh"), ("yl", "core")
    return jax.shard_map(
        body,
        mesh=fine,
        in_specs=(P(blk, dp), P(blk, dp), P(dp + blk, None), P(blk, None)),
        out_specs=(P(blk, None), P(dp + blk, None), P(blk, dp), P(blk, dp)),
        check_vma=False,
    )
```

```python
import functools

import jax
import jax.numpy as jnp
from jax import lax
from jax.experimental import pallas as pl
from jax.experimental.pallas import tpu as pltpu
from jax.sharding import Mesh, PartitionSpec as P

BF16 = jnp.bfloat16
F32 = jnp.float32
NX, NZ = 4, 8
SLOT = 64
SENT = 56
TILE = 256


def shift(value, axis, steps):
    count = lax.axis_size(axis)
    return lax.ppermute(value, axis, [(i, (i + steps) % count) for i in range(count)])


def after(value, *others):
    return lax.optimization_barrier((value, others))[0]


def call(kernel, outs, *args, scratch=(), limit=24, flops=0, moved=None, space=pltpu.VMEM, out_space=pltpu.VMEM):
    if moved is None:
        moved = sum(a.size * a.dtype.itemsize for a in args + tuple(outs))
    return pl.pallas_call(
        kernel,
        out_shape=outs,
        in_specs=[pl.BlockSpec(memory_space=space)] * len(args),
        out_specs=[pl.BlockSpec(memory_space=out_space)] * len(outs),
        scratch_shapes=list(scratch),
        compiler_params=pltpu.CompilerParams(vmem_limit_bytes=limit * 2**20),
        cost_estimate=pl.CostEstimate(flops=flops, bytes_accessed=moved, transcendentals=0),
    )(*args)


def like(shape, dtype=BF16):
    return jax.ShapeDtypeStruct(shape, dtype)


def store_swapped(core, out, value):
    half = value.shape[1] // 2

    @pl.when(core == 0)
    def _():
        out[...] = value

    @pl.when(core != 0)
    def _():
        out[:, :half] = value[:, half:]
        out[:, half:] = value[:, :half]


def pack_weight(mine, other, out):
    rows = mine.shape[0]
    yh = lax.axis_index("yh")
    to = lax.broadcasted_iota(jnp.int32, (SENT, rows), 0)
    row = lax.broadcasted_iota(jnp.int32, (SENT, rows), 1)
    place = jnp.where(to == row + rows * yh, 1.0, 0.0).astype(BF16)
    place_other = jnp.where(to == row + rows * (1 - yh), 1.0, 0.0).astype(BF16)
    both = jnp.dot(place, mine[...], preferred_element_type=F32)
    both = both + jnp.dot(place_other, other[...], preferred_element_type=F32)
    store_swapped(lax.axis_index("core"), out, both.astype(BF16))


def prepare(gate_hbm, up_hbm, cot_hbm, m1, m2, m3, hid_own, cot, gate, up, hidden, slots, sems):
    units, rows = gate.shape
    half = cot_hbm.shape[1] // 2
    part = units // NX
    used = part // NZ
    x, core = lax.axis_index("x"), lax.axis_index("core")
    started = []

    def copy(source, to):
        started.append(pltpu.make_async_copy(source, to, sems.at[len(started)]))
        started[-1].start()
        return started[-1]

    cot_loads = []
    for s in range(NX):
        here = pl.ds(s * (rows // NX), rows // NX)
        cot_loads.append(copy(cot_hbm.at[here], cot.at[here]))
    loads = []
    for s in range(NX):
        here = pl.ds(s * part, part)
        loads.append([copy(gate_hbm.at[here], gate.at[here]), copy(up_hbm.at[here], up.at[here])])
    for load in cot_loads:
        load.wait()
    mine = cot.at[:, pl.ds(pl.multiple_of(core * half, half), half)]
    for out in (m1, m3):
        copy(mine, out.at[:, pl.ds(0, half)])
    quarter = half // 2
    start = pl.multiple_of(core * half + lax.axis_index("yl") * quarter, quarter)
    copy(cot.at[:, pl.ds(start, quarter)], m2.at[:, pl.ds(0, quarter)])
    inside = lax.broadcasted_iota(jnp.int32, (SLOT, rows), 0) < used
    for s in range(NX):
        for load in loads[s]:
            load.wait()
        here = slice(s * part, (s + 1) * part)
        gate32, up32 = gate[here].astype(F32), up[here].astype(F32)
        hidden[here] = (gate32 * jax.nn.sigmoid(gate32) * up32).astype(BF16).astype(F32)
        for block in range(NZ):
            start = s * part + used * block
            value = jnp.where(inside, hidden[start : start + SLOT], 0.0).astype(BF16)
            row, column = block * SLOT % rows, block * SLOT // rows * rows
            slots[s, row : row + SLOT, column : column + rows] = value
    for k, out in enumerate((m1, m2, m3)):
        start = out.shape[1] - NZ * SLOT
        copy(slots.at[lax.rem(x + k + 1, NX)], out.at[:, pl.ds(start, NZ * SLOT)])
    for i in range(NZ * SLOT // rows):
        here = pl.ds(i * rows, rows)
        copy(slots.at[x, :, here], hid_own.at[here])
    for last in started[3 * NX :]:
        last.wait()


def near_halves(g1, g2, g3, swapped2, n1, n2, n3):
    half = n1.shape[1]
    quarter = half // 2
    n1[...] = g1[:, :half]
    n3[...] = g3[:, :half]

    @pl.when(lax.axis_index("yl") == 0)
    def _():
        n2[:, :quarter] = g2[:, :quarter]
        n2[:, quarter:] = swapped2[:, :quarter]

    @pl.when(lax.axis_index("yl") != 0)
    def _():
        n2[:, :quarter] = swapped2[:, :quarter]
        n2[:, quarter:] = g2[:, :quarter]


def add_up(own, h1, h2, h3, out):
    quarter = h2.shape[1]
    low = lax.axis_index("yl") == 0
    total = own[...] + h1[...].astype(F32) + h3[...].astype(F32)
    more = h2[...].astype(F32)

    @pl.when(low)
    def _():
        out[:, :quarter] = (total[:, :quarter] + more).astype(BF16)
        out[:, quarter:] = total[:, quarter:].astype(BF16)

    @pl.when(jnp.logical_not(low))
    def _():
        out[:, :quarter] = total[:, :quarter].astype(BF16)
        out[:, quarter:] = (total[:, quarter:] + more).astype(BF16)


def weight_gradient(scale, cot_own, hid_own, g1, g2, g3, n2, f1, f2, f3, pieces, to_bwd, cot, hid, hid_t):
    rows, half = cot_own.shape[0], cot_own.shape[1] // 2
    store_swapped(lax.axis_index("core"), cot.at[:rows], cot_own[...])
    hid_t[:, :rows] = hid_own[...]
    for k, (got, near, far) in enumerate(((g1, g1, f1), (g2, n2, f2), (g3, g3, f3))):
        here = slice((k + 1) * rows, (k + 2) * rows)
        cot[here, :half] = near[:, :half]
        cot[here, half:] = far[...]
        for i in range(NZ * SLOT // rows):
            from_column = got.shape[1] - NZ * SLOT + i * rows
            hid_t[i * rows : (i + 1) * rows, here] = got[:, from_column : from_column + rows]
    z = lax.axis_index("z")

    @pl.loop(0, cot.shape[1] // TILE)
    def _(t):
        columns = pl.ds(pl.multiple_of(t * TILE, TILE), TILE)
        product = jnp.dot(hid_t[...], cot[:, columns], preferred_element_type=F32) * scale
        for block in range(NZ):
            distance = lax.rem(block - z + NZ, NZ)
            pieces[distance, :, columns] = product[block * SLOT : block * SLOT + SENT]

    to_bwd[...] = pieces[NZ // 2].astype(BF16)
    hid[...] = hid_t[...].T


def padded(piece):
    rows, width = piece.shape
    return jnp.concatenate([piece[...].astype(F32), jnp.zeros((SLOT - rows, width), F32)], 0).astype(BF16)


def near_blocks(w0, f1, f2, f3, b3, b2, b1, hid, weight, product, opposite, other, mark):
    z = lax.axis_index("z")
    width = w0.shape[1]
    half = width // 2
    for distance, piece in enumerate((w0, f1, f2, f3, None, b3, b2, b1)):
        to = lax.rem(z - distance + NZ, NZ)
        if piece is None:
            weight[to] = jnp.zeros((SLOT, width), BF16)
        else:
            weight[to] = padded(piece)

    @pl.loop(0, half // TILE)
    def _(t):
        here = pl.ds(pl.multiple_of(t * TILE, TILE), TILE)
        there = pl.ds(pl.multiple_of(half + t * TILE, TILE), TILE)
        rhs = weight[:, :, there].reshape(NZ * SLOT, TILE)
        other[:, here] = jnp.dot(hid[...], rhs, preferred_element_type=F32).astype(BF16)
        rhs = weight[:, :, here].reshape(NZ * SLOT, TILE)
        product[:, here] = jnp.dot(hid[...], rhs, preferred_element_type=F32)

    for block in range(NZ):

        @pl.when(z == (block + NZ // 2) % NZ)
        def _(block=block):
            some = hid[:, block * SLOT : (block + 1) * SLOT]
            opposite[...] = some
            other[:, half:] = jnp.concatenate([some, jnp.zeros_like(some)], 1)

    mark[...] = w0[: mark.shape[0], : mark.shape[1]]


def other_half(block, mark, out):
    out[...] = block[:, out.shape[1] :]


def output_parts(product, crossed, opposite, block, block_other, total, m1, m3, keep, give, second):
    rows, half = total.shape
    quarter = half // 2
    own, far = padded(block.at[:, :half]), padded(block_other)
    far_hidden = crossed[:, half : half + SLOT]
    for t in range(half // TILE):
        here = slice(t * TILE, (t + 1) * TILE)
        value = product[:, here] + crossed[:, here].astype(F32)
        value = value + jnp.dot(opposite[...], own[:, here], preferred_element_type=F32)
        value = value + jnp.dot(far_hidden, far[:, here], preferred_element_type=F32)
        total[:, here] = value[:rows]
        m1[:, here] = value[rows : 2 * rows].astype(BF16)
        second[:, here] = value[2 * rows : 3 * rows]
        m3[:, here] = value[3 * rows : 4 * rows].astype(BF16)

    @pl.when(lax.axis_index("yl") == 0)
    def _():
        keep[...] = second[:, :quarter]
        give[...] = second[:, quarter:].astype(BF16)

    @pl.when(lax.axis_index("yl") != 0)
    def _():
        keep[...] = second[:, quarter:]
        give[...] = second[:, :quarter].astype(BF16)


def first_rows(value, out):
    out[...] = value[: out.shape[0], : out.shape[1]]


def add_given(keep, given, out):
    out[...] = (keep[...] + given[...].astype(F32)).astype(BF16)


def back_parts(cot, weight, block, *parts):
    slots = TILE // SLOT
    rows = parts[0].shape[1]
    dims = (((1,), (1,)), ((), ()))

    @pl.loop(0, NZ // slots)
    def _(t):
        some = weight[pl.ds(t * slots, slots)].reshape(TILE, weight.shape[2])
        product = lax.dot_general(some, cot[...], dims, preferred_element_type=F32)
        for k, part in enumerate(parts):
            part[pl.ds(pl.multiple_of(t * TILE, TILE), TILE)] = product[
                :, k * rows : (k + 1) * rows
            ].astype(BF16)

    opposite = lax.rem(lax.axis_index("z") + NZ // 2, NZ)
    product = lax.dot_general(padded(block), cot[...], dims, preferred_element_type=F32)
    for k, part in enumerate(parts):
        part[pl.ds(pl.multiple_of(opposite * SLOT, SLOT), SLOT)] = product[
            :, k * rows : (k + 1) * rows
        ].astype(BF16)


def activation_gradients(gate, up, b0, b1, b2, b3, grad_gate, grad_up, back32):
    units, rows = gate.shape
    used = units // (NX * NZ)
    for x in range(NX):

        @pl.when(lax.axis_index("x") == x)
        def _(x=x):
            for s in range(NX):
                source = (b0, b1, b2, b3)[(s - x) % NX]
                for block in range(NZ):
                    value = source[block * SLOT : (block + 1) * SLOT].astype(F32)
                    start = (s * NZ + block) * used
                    back32[start : start + used] = value[:used]

    gate32, up32 = gate[...].astype(F32), up[...].astype(F32)
    sig = jax.nn.sigmoid(gate32)
    grad_gate[...] = (back32[...] * up32 * (sig * (1.0 + gate32 * (1.0 - sig)))).astype(BF16)
    grad_up[...] = (back32[...] * (gate32 * sig)).astype(BF16)


def add_pieces(distance, others, pieces, *refs):
    *sums, to_fwd, to_bwd = refs[others:]
    here = pieces[distance]
    if len(sums) > 1:
        here = here + sums[0][...].astype(F32)
    to_fwd[...] = here.astype(BF16)
    to_bwd[...] = (pieces[NZ - distance] + sums[-1][...].astype(F32)).astype(BF16)


def finish_rows(pieces, fwd, bwd, keep, give, total):
    rows, half = keep.shape[0], keep.shape[1] // 2
    core, yh = lax.axis_index("core"), lax.axis_index("yh")
    store_swapped(core, total, pieces[0] + (fwd[...].astype(F32) + bwd[...].astype(F32)))

    @pl.when(yh == 0)
    def _():
        keep[...] = total[:rows]
        give[...] = total[rows : 2 * rows].astype(BF16)

    @pl.when(yh != 0)
    def _():
        keep[...] = total[rows : 2 * rows]
        give[...] = total[:rows].astype(BF16)


def finish(mine, other, keep, taken, out, grad):
    half = mine.shape[1]

    @pl.when(lax.axis_index("core") == 0)
    def _():
        out[:, :half] = mine[...]
        out[:, half:] = other[...]

    @pl.when(lax.axis_index("core") != 0)
    def _():
        out[:, :half] = other[...]
        out[:, half:] = mine[...]

    grad[...] = keep[...] + taken[...].astype(F32)


def body(gate_pre, up_pre, down_weight, cotangent):
    gate, up = gate_pre.T, up_pre.T
    units, rows = gate.shape
    block, width = down_weight.shape
    half = width // 2
    slots = NZ * SLOT
    tokens = NX * rows
    wide = half + slots

    w_other = shift(down_weight, "yh", 1)
    m1, m2, m3, hid_own = call(
        prepare,
        [like((rows, wide)), like((rows, wide - half // 2)), like((rows, wide))]
        + [like((slots, rows))],
        gate, up, cotangent,
        scratch=[pltpu.VMEM((rows, width), BF16)]
        + [pltpu.VMEM((units, rows), BF16)] * 2
        + [pltpu.VMEM((units + SLOT, rows), F32), pltpu.VMEM((NX, rows, slots), BF16)]
        + [pltpu.SemaphoreType.DMA((3 * NX + 6 + slots // rows,))],
        out_space=pltpu.HBM,
        space=pltpu.HBM,
        limit=56,
    )
    w_other = after(w_other, m1, m2, m3)
    (w0,) = call(pack_weight, [like((SENT, width))], down_weight, w_other, flops=18 * 10**8)
    got = [shift(m, "x", k) for k, m in ((1, m1), (2, m2), (3, m3))]

    nears = call(
        near_halves,
        [like((rows, half))] * 3,
        *got, shift(got[1], "yl", 1),
        flops=200 * 10**6,
        moved=0,
    )
    far = [shift(near, "core", 1) for near in nears]

    fwd, bwd = [w0], [w0]
    for step in range(3):
        f, b = shift(fwd[-1], "z", 1), shift(bwd[-1], "z", -1)
        f, b = lax.optimization_barrier((f, b))
        fwd.append(f)
        bwd.append(b)
    scale = float(tokens * NZ * 2) ** (-0.5)
    pieces, to_bwd, cot, hid = call(
        functools.partial(weight_gradient, scale),
        [like((NZ, SENT, width), F32), like((SENT, width)), like((tokens, width)), like((tokens, slots))],
        cotangent, hid_own, *got, nears[1], *far,
        scratch=[pltpu.VMEM((slots, tokens), BF16)],
        flops=0,
        moved=0,
    )

    def added(distance, ring, *others):
        kernel = functools.partial(add_pieces, distance, len(others))
        return call(kernel, [like((SENT, width))] * 2, pieces, *others, *ring, moved=0)

    f4 = shift(fwd[3], "z", 1)
    ring = (shift(to_bwd, "z", -1),)

    weight, product, opposite, other, early = call(
        near_blocks,
        [like((NZ, SLOT, width)), like((tokens, half), F32), like((tokens, SLOT))]
        + [like((tokens, half + 2 * SLOT)), like((16, 128))],
        *fwd, *reversed(bwd[1:]), hid,
        moved=0,
    )
    crossed = shift(other, "core", 1)
    to_fwd, to_bwd = added(3, ring, early)
    ring = (shift(to_fwd, "z", 1), shift(to_bwd, "z", -1))

    (mark,) = call(first_rows, [like((16, 128))], to_fwd, flops=2 * 10**9)
    (block_half,) = call(other_half, [like((SENT, half))], f4, mark, flops=14 * 10**9)
    total, m1, m3, keep2, give2 = call(
        output_parts,
        [like((rows, half), F32)] + [like((rows, half))] * 2
        + [like((rows, half // 2), F32), like((rows, half // 2))],
        product, crossed, opposite, f4, shift(block_half, "core", 1),
        scratch=[pltpu.VMEM((rows, half), F32)],
        flops=1 * 10**9,
        moved=0,
    )
    given2 = shift(give2, "yl", 1)
    got1, got3 = shift(m1, "x", -1), shift(m3, "x", -3)
    (m2,) = call(add_given, [like((rows, half // 2))], keep2, given2, moved=0)
    got_out = [got1, shift(m2, "x", -2), got3]
    back_own, *backs = call(
        back_parts, [like((slots, rows))] * NX, after(cot, m1), weight, f4, moved=0
    )
    back1, back2, back3 = backs
    ring = after(ring, m1, m3)
    to_fwd, to_bwd = added(2, ring)
    ring = (shift(to_fwd, "z", 1), shift(to_bwd, "z", -1))
    *ring, back1, back2, back3 = lax.optimization_barrier((*ring, back1, back2, back3))
    got_back1, got_back3 = shift(back1, "x", -1), shift(back3, "x", -3)
    to_fwd, to_bwd = added(1, ring)
    got_out = after(got_out, to_fwd, to_bwd)
    ring = (shift(to_fwd, "z", 1), shift(to_bwd, "z", -1))
    (rounded,) = call(add_up, [like((rows, half))], total, *got_out, moved=0)
    across = shift(rounded, "yl", 1)
    ring = after(ring, rounded)
    keep, give = call(
        finish_rows,
        [like((block, width), F32), like((block, width))],
        pieces, *ring,
        scratch=[pltpu.VMEM((SENT, width), F32)],
        flops=60 * 10**7,
        moved=0,
    )
    taken = shift(give, "yh", 1)
    got_back2 = shift(after(back2, give), "x", -2)
    grad_gate, grad_up = call(
        activation_gradients,
        [like((units, rows))] * 2,
        gate, up, back_own, got_back1, got_back2, got_back3,
        scratch=[pltpu.VMEM((units, rows), F32)],
        flops=400 * 10**7,
        moved=0,
    )
    across = after(across, give)
    out_half = (rounded.astype(F32) + across.astype(F32)).astype(BF16)
    output, grad_weight = call(
        finish,
        [like((rows, width)), like((block, width), F32)],
        out_half, shift(out_half, "core", 1), keep, taken,
    )
    return output, grad_weight, grad_gate.T, grad_up.T


def solution(mesh):
    fine = Mesh(mesh.devices.reshape(2, 2, NX, NZ, 2), ("yl", "core", "x", "z", "yh"))
    blk, dp = ("x", "z", "yh"), ("yl", "core")
    return jax.shard_map(
        body,
        mesh=fine,
        in_specs=(P(blk, dp), P(blk, dp), P(dp + blk, None), P(blk, None)),
        out_specs=(P(blk, None), P(dp + blk, None), P(blk, dp), P(blk, dp)),
        check_vma=False,
    )
```

```python
import functools

import jax
import jax.numpy as jnp
from jax import lax
from jax.experimental import pallas as pl
from jax.experimental.pallas import tpu as pltpu
from jax.sharding import Mesh, PartitionSpec as P

BF16 = jnp.bfloat16
F32 = jnp.float32
NX, NZ = 4, 8
SLOT = 64
SENT = 56
TILE = 256


def shift(value, axis, steps):
    count = lax.axis_size(axis)
    return lax.ppermute(value, axis, [(i, (i + steps) % count) for i in range(count)])


def after(value, *others):
    return lax.optimization_barrier((value, others))[0]


def call(kernel, outs, *args, scratch=(), limit=24, flops=0, moved=None, space=pltpu.VMEM, out_space=pltpu.VMEM):
    if moved is None:
        moved = sum(a.size * a.dtype.itemsize for a in args + tuple(outs))
    return pl.pallas_call(
        kernel,
        out_shape=outs,
        in_specs=[pl.BlockSpec(memory_space=space)] * len(args),
        out_specs=[pl.BlockSpec(memory_space=out_space)] * len(outs),
        scratch_shapes=list(scratch),
        compiler_params=pltpu.CompilerParams(vmem_limit_bytes=limit * 2**20),
        cost_estimate=pl.CostEstimate(flops=flops, bytes_accessed=moved, transcendentals=0),
    )(*args)


def like(shape, dtype=BF16):
    return jax.ShapeDtypeStruct(shape, dtype)


def store_swapped(core, out, value):
    half = value.shape[1] // 2

    @pl.when(core == 0)
    def _():
        out[...] = value

    @pl.when(core != 0)
    def _():
        out[:, :half] = value[:, half:]
        out[:, half:] = value[:, :half]


def pack_weight(mine, other, out):
    rows = mine.shape[0]
    yh = lax.axis_index("yh")
    to = lax.broadcasted_iota(jnp.int32, (SENT, rows), 0)
    row = lax.broadcasted_iota(jnp.int32, (SENT, rows), 1)
    place = jnp.where(to == row + rows * yh, 1.0, 0.0).astype(BF16)
    place_other = jnp.where(to == row + rows * (1 - yh), 1.0, 0.0).astype(BF16)
    both = jnp.dot(place, mine[...], preferred_element_type=F32)
    both = both + jnp.dot(place_other, other[...], preferred_element_type=F32)
    store_swapped(lax.axis_index("core"), out, both.astype(BF16))


def prepare(gate_hbm, up_hbm, cot_hbm, m1, m2, m3, hid_own, cot, gate, up, hidden, slots, sems):
    units, rows = gate.shape
    half = cot_hbm.shape[1] // 2
    part = units // NX
    used = part // NZ
    x, core = lax.axis_index("x"), lax.axis_index("core")
    started = []

    def copy(source, to):
        started.append(pltpu.make_async_copy(source, to, sems.at[len(started)]))
        started[-1].start()
        return started[-1]

    cot_loads = []
    for s in range(NX):
        here = pl.ds(s * (rows // NX), rows // NX)
        cot_loads.append(copy(cot_hbm.at[here], cot.at[here]))
    loads = []
    for s in range(NX):
        here = pl.ds(s * part, part)
        loads.append([copy(gate_hbm.at[here], gate.at[here]), copy(up_hbm.at[here], up.at[here])])
    for load in cot_loads:
        load.wait()
    mine = cot.at[:, pl.ds(pl.multiple_of(core * half, half), half)]
    for out in (m1, m3):
        copy(mine, out.at[:, pl.ds(0, half)])
    quarter = half // 2
    start = pl.multiple_of(core * half + lax.axis_index("yl") * quarter, quarter)
    copy(cot.at[:, pl.ds(start, quarter)], m2.at[:, pl.ds(0, quarter)])
    inside = lax.broadcasted_iota(jnp.int32, (SLOT, rows), 0) < used
    for s in range(NX):
        for load in loads[s]:
            load.wait()
        here = slice(s * part, (s + 1) * part)
        gate32, up32 = gate[here].astype(F32), up[here].astype(F32)
        hidden[here] = (gate32 * jax.nn.sigmoid(gate32) * up32).astype(BF16).astype(F32)
        for block in range(NZ):
            start = s * part + used * block
            value = jnp.where(inside, hidden[start : start + SLOT], 0.0).astype(BF16)
            row, column = block * SLOT % rows, block * SLOT // rows * rows
            slots[s, row : row + SLOT, column : column + rows] = value
    for k, out in enumerate((m1, m2, m3)):
        start = out.shape[1] - NZ * SLOT
        copy(slots.at[lax.rem(x + k + 1, NX)], out.at[:, pl.ds(start, NZ * SLOT)])
    for i in range(NZ * SLOT // rows):
        here = pl.ds(i * rows, rows)
        copy(slots.at[x, :, here], hid_own.at[here])
    for last in started[3 * NX :]:
        last.wait()


def near_halves(g1, g2, g3, swapped2, n1, n2, n3):
    half = n1.shape[1]
    quarter = half // 2
    n1[...] = g1[:, :half]
    n3[...] = g3[:, :half]

    @pl.when(lax.axis_index("yl") == 0)
    def _():
        n2[:, :quarter] = g2[:, :quarter]
        n2[:, quarter:] = swapped2[:, :quarter]

    @pl.when(lax.axis_index("yl") != 0)
    def _():
        n2[:, :quarter] = swapped2[:, :quarter]
        n2[:, quarter:] = g2[:, :quarter]


def add_up(own, h1, h2, h3, out):
    quarter = h2.shape[1]
    low = lax.axis_index("yl") == 0
    total = own[...] + h1[...].astype(F32) + h3[...].astype(F32)
    more = h2[...].astype(F32)

    @pl.when(low)
    def _():
        out[:, :quarter] = (total[:, :quarter] + more).astype(BF16)
        out[:, quarter:] = total[:, quarter:].astype(BF16)

    @pl.when(jnp.logical_not(low))
    def _():
        out[:, :quarter] = total[:, :quarter].astype(BF16)
        out[:, quarter:] = (total[:, quarter:] + more).astype(BF16)


def weight_gradient(scale, cot_own, hid_own, g1, g2, g3, n2, f1, f2, f3, pieces, to_bwd, cot, hid, hid_t):
    rows, half = cot_own.shape[0], cot_own.shape[1] // 2
    store_swapped(lax.axis_index("core"), cot.at[:rows], cot_own[...])
    hid_t[:, :rows] = hid_own[...]
    for k, (got, near, far) in enumerate(((g1, g1, f1), (g2, n2, f2), (g3, g3, f3))):
        here = slice((k + 1) * rows, (k + 2) * rows)
        cot[here, :half] = near[:, :half]
        cot[here, half:] = far[...]
        for i in range(NZ * SLOT // rows):
            from_column = got.shape[1] - NZ * SLOT + i * rows
            hid_t[i * rows : (i + 1) * rows, here] = got[:, from_column : from_column + rows]
    z = lax.axis_index("z")

    @pl.loop(0, cot.shape[1] // TILE)
    def _(t):
        columns = pl.ds(pl.multiple_of(t * TILE, TILE), TILE)
        product = jnp.dot(hid_t[...], cot[:, columns], preferred_element_type=F32) * scale
        for block in range(NZ):
            distance = lax.rem(block - z + NZ, NZ)
            pieces[distance, :, columns] = product[block * SLOT : block * SLOT + SENT]

    to_bwd[...] = pieces[NZ // 2].astype(BF16)
    hid[...] = hid_t[...].T


def padded(piece):
    rows, width = piece.shape
    return jnp.concatenate([piece[...].astype(F32), jnp.zeros((SLOT - rows, width), F32)], 0).astype(BF16)


def near_blocks(w0, f1, f2, f3, b3, b2, b1, hid, weight, product, opposite, other, mark):
    z = lax.axis_index("z")
    width = w0.shape[1]
    half = width // 2
    for distance, piece in enumerate((w0, f1, f2, f3, None, b3, b2, b1)):
        to = lax.rem(z - distance + NZ, NZ)
        if piece is None:
            weight[to] = jnp.zeros((SLOT, width), BF16)
        else:
            weight[to] = padded(piece)

    @pl.loop(0, half // TILE)
    def _(t):
        here = pl.ds(pl.multiple_of(t * TILE, TILE), TILE)
        there = pl.ds(pl.multiple_of(half + t * TILE, TILE), TILE)
        rhs = weight[:, :, there].reshape(NZ * SLOT, TILE)
        other[:, here] = jnp.dot(hid[...], rhs, preferred_element_type=F32).astype(BF16)
        rhs = weight[:, :, here].reshape(NZ * SLOT, TILE)
        product[:, here] = jnp.dot(hid[...], rhs, preferred_element_type=F32)

    for block in range(NZ):

        @pl.when(z == (block + NZ // 2) % NZ)
        def _(block=block):
            some = hid[:, block * SLOT : (block + 1) * SLOT]
            opposite[...] = some
            other[:, half:] = jnp.concatenate([some, jnp.zeros_like(some)], 1)

    mark[...] = w0[: mark.shape[0], : mark.shape[1]]


def other_half(block, mark, out):
    out[...] = block[:, out.shape[1] :]


def output_parts(product, crossed, opposite, block, block_other, total, m1, m3, keep, give, second):
    rows, half = total.shape
    quarter = half // 2
    own, far = padded(block.at[:, :half]), padded(block_other)
    far_hidden = crossed[:, half : half + SLOT]
    for t in range(half // TILE):
        here = slice(t * TILE, (t + 1) * TILE)
        value = product[:, here] + crossed[:, here].astype(F32)
        value = value + jnp.dot(opposite[...], own[:, here], preferred_element_type=F32)
        value = value + jnp.dot(far_hidden, far[:, here], preferred_element_type=F32)
        total[:, here] = value[:rows]
        m1[:, here] = value[rows : 2 * rows].astype(BF16)
        second[:, here] = value[2 * rows : 3 * rows]
        m3[:, here] = value[3 * rows : 4 * rows].astype(BF16)

    @pl.when(lax.axis_index("yl") == 0)
    def _():
        keep[...] = second[:, :quarter]
        give[...] = second[:, quarter:].astype(BF16)

    @pl.when(lax.axis_index("yl") != 0)
    def _():
        keep[...] = second[:, quarter:]
        give[...] = second[:, :quarter].astype(BF16)


def first_rows(value, out):
    out[...] = value[: out.shape[0], : out.shape[1]]


def add_given(keep, given, out):
    out[...] = (keep[...] + given[...].astype(F32)).astype(BF16)


def back_parts(cot, weight, block, *parts):
    slots = TILE // SLOT
    rows = parts[0].shape[1]
    dims = (((1,), (1,)), ((), ()))

    @pl.loop(0, NZ // slots)
    def _(t):
        some = weight[pl.ds(t * slots, slots)].reshape(TILE, weight.shape[2])
        product = lax.dot_general(some, cot[...], dims, preferred_element_type=F32)
        for k, part in enumerate(parts):
            part[pl.ds(pl.multiple_of(t * TILE, TILE), TILE)] = product[
                :, k * rows : (k + 1) * rows
            ].astype(BF16)

    opposite = lax.rem(lax.axis_index("z") + NZ // 2, NZ)
    product = lax.dot_general(padded(block), cot[...], dims, preferred_element_type=F32)
    for k, part in enumerate(parts):
        part[pl.ds(pl.multiple_of(opposite * SLOT, SLOT), SLOT)] = product[
            :, k * rows : (k + 1) * rows
        ].astype(BF16)


def activation_gradients(gate, up, b0, b1, b2, b3, grad_gate, grad_up, back32):
    units, rows = gate.shape
    used = units // (NX * NZ)
    for x in range(NX):

        @pl.when(lax.axis_index("x") == x)
        def _(x=x):
            for s in range(NX):
                source = (b0, b1, b2, b3)[(s - x) % NX]
                for block in range(NZ):
                    value = source[block * SLOT : (block + 1) * SLOT].astype(F32)
                    start = (s * NZ + block) * used
                    back32[start : start + used] = value[:used]

    gate32, up32 = gate[...].astype(F32), up[...].astype(F32)
    sig = jax.nn.sigmoid(gate32)
    grad_gate[...] = (back32[...] * up32 * (sig * (1.0 + gate32 * (1.0 - sig)))).astype(BF16)
    grad_up[...] = (back32[...] * (gate32 * sig)).astype(BF16)


def add_pieces(distance, others, pieces, *refs):
    *sums, to_fwd, to_bwd = refs[others:]
    here = pieces[distance]
    if len(sums) > 1:
        here = here + sums[0][...].astype(F32)
    to_fwd[...] = here.astype(BF16)
    to_bwd[...] = (pieces[NZ - distance] + sums[-1][...].astype(F32)).astype(BF16)


def finish_rows(pieces, fwd, bwd, keep, give, total):
    rows, half = keep.shape[0], keep.shape[1] // 2
    core, yh = lax.axis_index("core"), lax.axis_index("yh")
    store_swapped(core, total, pieces[0] + (fwd[...].astype(F32) + bwd[...].astype(F32)))

    @pl.when(yh == 0)
    def _():
        keep[...] = total[:rows]
        give[...] = total[rows : 2 * rows].astype(BF16)

    @pl.when(yh != 0)
    def _():
        keep[...] = total[rows : 2 * rows]
        give[...] = total[:rows].astype(BF16)


def finish(mine, other, keep, taken, out, grad):
    half = mine.shape[1]

    @pl.when(lax.axis_index("core") == 0)
    def _():
        out[:, :half] = mine[...]
        out[:, half:] = other[...]

    @pl.when(lax.axis_index("core") != 0)
    def _():
        out[:, :half] = other[...]
        out[:, half:] = mine[...]

    grad[...] = keep[...] + taken[...].astype(F32)


def body(gate_pre, up_pre, down_weight, cotangent):
    gate, up = gate_pre.T, up_pre.T
    units, rows = gate.shape
    block, width = down_weight.shape
    half = width // 2
    slots = NZ * SLOT
    tokens = NX * rows
    wide = half + slots

    w_other = shift(down_weight, "yh", 1)
    m1, m2, m3, hid_own = call(
        prepare,
        [like((rows, wide)), like((rows, wide - half // 2)), like((rows, wide))]
        + [like((slots, rows))],
        gate, up, cotangent,
        scratch=[pltpu.VMEM((rows, width), BF16)]
        + [pltpu.VMEM((units, rows), BF16)] * 2
        + [pltpu.VMEM((units + SLOT, rows), F32), pltpu.VMEM((NX, rows, slots), BF16)]
        + [pltpu.SemaphoreType.DMA((3 * NX + 6 + slots // rows,))],
        out_space=pltpu.HBM,
        space=pltpu.HBM,
        limit=56,
    )
    w_other = after(w_other, m1, m2, m3)
    (w0,) = call(pack_weight, [like((SENT, width))], down_weight, w_other, flops=18 * 10**8)
    got = [shift(m, "x", k) for k, m in ((1, m1), (2, m2), (3, m3))]

    nears = call(
        near_halves,
        [like((rows, half))] * 3,
        *got, shift(got[1], "yl", 1),
        flops=200 * 10**6,
        moved=0,
    )
    far = [shift(near, "core", 1) for near in nears]

    fwd, bwd = [w0], [w0]
    for step in range(3):
        f, b = shift(fwd[-1], "z", 1), shift(bwd[-1], "z", -1)
        f, b = lax.optimization_barrier((f, b))
        fwd.append(f)
        bwd.append(b)
    scale = float(tokens * NZ * 2) ** (-0.5)
    pieces, to_bwd, cot, hid = call(
        functools.partial(weight_gradient, scale),
        [like((NZ, SENT, width), F32), like((SENT, width)), like((tokens, width)), like((tokens, slots))],
        cotangent, hid_own, *got, nears[1], *far,
        scratch=[pltpu.VMEM((slots, tokens), BF16)],
        flops=0,
        moved=0,
    )

    def added(distance, ring, *others):
        kernel = functools.partial(add_pieces, distance, len(others))
        return call(kernel, [like((SENT, width))] * 2, pieces, *others, *ring, moved=0)

    f4 = shift(fwd[3], "z", 1)
    ring = (shift(to_bwd, "z", -1),)

    weight, product, opposite, other, early = call(
        near_blocks,
        [like((NZ, SLOT, width)), like((tokens, half), F32), like((tokens, SLOT))]
        + [like((tokens, half + 2 * SLOT)), like((16, 128))],
        *fwd, *reversed(bwd[1:]), hid,
        moved=0,
    )
    crossed = shift(other, "core", 1)
    to_fwd, to_bwd = added(3, ring, early)
    ring = (shift(to_fwd, "z", 1), shift(to_bwd, "z", -1))

    (mark,) = call(first_rows, [like((16, 128))], to_fwd, flops=2 * 10**9)
    (block_half,) = call(other_half, [like((SENT, half))], f4, mark, flops=14 * 10**9)
    total, m1, m3, keep2, give2 = call(
        output_parts,
        [like((rows, half), F32)] + [like((rows, half))] * 2
        + [like((rows, half // 2), F32), like((rows, half // 2))],
        product, crossed, opposite, f4, shift(block_half, "core", 1),
        scratch=[pltpu.VMEM((rows, half), F32)],
        flops=1 * 10**9,
        moved=0,
    )
    given2 = shift(give2, "yl", 1)
    got1, got3 = shift(m1, "x", -1), shift(m3, "x", -3)
    (m2,) = call(add_given, [like((rows, half // 2))], keep2, given2, moved=0)
    got_out = [got1, shift(m2, "x", -2), got3]
    back_own, *backs = call(
        back_parts, [like((slots, rows))] * NX, after(cot, m1), weight, f4, moved=0
    )
    back1, back2, back3 = backs
    ring = after(ring, m1, m3)
    to_fwd, to_bwd = added(2, ring)
    ring = (shift(to_fwd, "z", 1), shift(to_bwd, "z", -1))
    *ring, back1, back2, back3 = lax.optimization_barrier((*ring, back1, back2, back3))
    got_back1, got_back2 = shift(back1, "x", -1), shift(back2, "x", -2)
    to_fwd, to_bwd = added(1, ring)
    got_out = after(got_out, to_fwd, to_bwd)
    ring = (shift(to_fwd, "z", 1), shift(to_bwd, "z", -1))
    (rounded,) = call(add_up, [like((rows, half))], total, *got_out, moved=0)
    across = shift(rounded, "yl", 1)
    ring = after(ring, rounded)
    keep, give = call(
        finish_rows,
        [like((block, width), F32), like((block, width))],
        pieces, *ring,
        scratch=[pltpu.VMEM((SENT, width), F32)],
        flops=60 * 10**7,
        moved=0,
    )
    taken = shift(give, "yh", 1)
    got_back3 = shift(after(back3, give), "x", -3)
    grad_gate, grad_up = call(
        activation_gradients,
        [like((units, rows))] * 2,
        gate, up, back_own, got_back1, got_back2, got_back3,
        scratch=[pltpu.VMEM((units, rows), F32)],
        flops=400 * 10**7,
        moved=0,
    )
    across = after(across, give)
    out_half = (rounded.astype(F32) + across.astype(F32)).astype(BF16)
    output, grad_weight = call(
        finish,
        [like((rows, width)), like((block, width), F32)],
        out_half, shift(out_half, "core", 1), keep, taken,
    )
    return output, grad_weight, grad_gate.T, grad_up.T


def solution(mesh):
    fine = Mesh(mesh.devices.reshape(2, 2, NX, NZ, 2), ("yl", "core", "x", "z", "yh"))
    blk, dp = ("x", "z", "yh"), ("yl", "core")
    return jax.shard_map(
        body,
        mesh=fine,
        in_specs=(P(blk, dp), P(blk, dp), P(dp + blk, None), P(blk, None)),
        out_specs=(P(blk, None), P(dp + blk, None), P(blk, dp), P(blk, dp)),
        check_vma=False,
    )
```

```python
import functools

import jax
import jax.numpy as jnp
from jax import lax
from jax.experimental import pallas as pl
from jax.experimental.pallas import tpu as pltpu
from jax.sharding import Mesh, PartitionSpec as P

BF16 = jnp.bfloat16
F32 = jnp.float32
NX, NZ = 4, 8
SLOT = 64
SENT = 56
TILE = 256


def shift(value, axis, steps):
    count = lax.axis_size(axis)
    return lax.ppermute(value, axis, [(i, (i + steps) % count) for i in range(count)])


def after(value, *others):
    return lax.optimization_barrier((value, others))[0]


def call(kernel, outs, *args, scratch=(), limit=24, flops=0, moved=None, space=pltpu.VMEM, out_space=pltpu.VMEM):
    if moved is None:
        moved = sum(a.size * a.dtype.itemsize for a in args + tuple(outs))
    return pl.pallas_call(
        kernel,
        out_shape=outs,
        in_specs=[pl.BlockSpec(memory_space=space)] * len(args),
        out_specs=[pl.BlockSpec(memory_space=out_space)] * len(outs),
        scratch_shapes=list(scratch),
        compiler_params=pltpu.CompilerParams(vmem_limit_bytes=limit * 2**20),
        cost_estimate=pl.CostEstimate(flops=flops, bytes_accessed=moved, transcendentals=0),
    )(*args)


def like(shape, dtype=BF16):
    return jax.ShapeDtypeStruct(shape, dtype)


def store_swapped(core, out, value):
    half = value.shape[1] // 2

    @pl.when(core == 0)
    def _():
        out[...] = value

    @pl.when(core != 0)
    def _():
        out[:, :half] = value[:, half:]
        out[:, half:] = value[:, :half]


def pack_weight(mine, other, out):
    rows = mine.shape[0]
    yh = lax.axis_index("yh")
    to = lax.broadcasted_iota(jnp.int32, (SENT, rows), 0)
    row = lax.broadcasted_iota(jnp.int32, (SENT, rows), 1)
    place = jnp.where(to == row + rows * yh, 1.0, 0.0).astype(BF16)
    place_other = jnp.where(to == row + rows * (1 - yh), 1.0, 0.0).astype(BF16)
    both = jnp.dot(place, mine[...], preferred_element_type=F32)
    both = both + jnp.dot(place_other, other[...], preferred_element_type=F32)
    store_swapped(lax.axis_index("core"), out, both.astype(BF16))


def prepare(gate_hbm, up_hbm, cot_hbm, m1, m2, m3, hid_own, cot, gate, up, hidden, slots, sems):
    units, rows = gate.shape
    half = cot_hbm.shape[1] // 2
    part = units // NX
    used = part // NZ
    x, core = lax.axis_index("x"), lax.axis_index("core")
    started = []

    def copy(source, to):
        started.append(pltpu.make_async_copy(source, to, sems.at[len(started)]))
        started[-1].start()
        return started[-1]

    cot_loads = []
    for s in range(NX):
        here = pl.ds(s * (rows // NX), rows // NX)
        cot_loads.append(copy(cot_hbm.at[here], cot.at[here]))
    loads = []
    for s in range(NX):
        here = pl.ds(s * part, part)
        loads.append([copy(gate_hbm.at[here], gate.at[here]), copy(up_hbm.at[here], up.at[here])])
    for load in cot_loads:
        load.wait()
    mine = cot.at[:, pl.ds(pl.multiple_of(core * half, half), half)]
    for out in (m1, m3):
        copy(mine, out.at[:, pl.ds(0, half)])
    quarter = half // 2
    start = pl.multiple_of(core * half + lax.axis_index("yl") * quarter, quarter)
    copy(cot.at[:, pl.ds(start, quarter)], m2.at[:, pl.ds(0, quarter)])
    inside = lax.broadcasted_iota(jnp.int32, (SLOT, rows), 0) < used
    for s in range(NX):
        for load in loads[s]:
            load.wait()
        here = slice(s * part, (s + 1) * part)
        gate32, up32 = gate[here].astype(F32), up[here].astype(F32)
        hidden[here] = (gate32 * jax.nn.sigmoid(gate32) * up32).astype(BF16).astype(F32)
        for block in range(NZ):
            start = s * part + used * block
            value = jnp.where(inside, hidden[start : start + SLOT], 0.0).astype(BF16)
            row, column = block * SLOT % rows, block * SLOT // rows * rows
            slots[s, row : row + SLOT, column : column + rows] = value
    for k, out in enumerate((m1, m2, m3)):
        start = out.shape[1] - NZ * SLOT
        copy(slots.at[lax.rem(x + k + 1, NX)], out.at[:, pl.ds(start, NZ * SLOT)])
    for i in range(NZ * SLOT // rows):
        here = pl.ds(i * rows, rows)
        copy(slots.at[x, :, here], hid_own.at[here])
    for last in started[3 * NX :]:
        last.wait()


def near_halves(g1, g2, g3, swapped2, n1, n2, n3):
    half = n1.shape[1]
    quarter = half // 2
    n1[...] = g1[:, :half]
    n3[...] = g3[:, :half]

    @pl.when(lax.axis_index("yl") == 0)
    def _():
        n2[:, :quarter] = g2[:, :quarter]
        n2[:, quarter:] = swapped2[:, :quarter]

    @pl.when(lax.axis_index("yl") != 0)
    def _():
        n2[:, :quarter] = swapped2[:, :quarter]
        n2[:, quarter:] = g2[:, :quarter]


def add_up(own, h1, h2, h3, out):
    quarter = h2.shape[1]
    low = lax.axis_index("yl") == 0
    total = own[...] + h1[...].astype(F32) + h3[...].astype(F32)
    more = h2[...].astype(F32)

    @pl.when(low)
    def _():
        out[:, :quarter] = (total[:, :quarter] + more).astype(BF16)
        out[:, quarter:] = total[:, quarter:].astype(BF16)

    @pl.when(jnp.logical_not(low))
    def _():
        out[:, :quarter] = total[:, :quarter].astype(BF16)
        out[:, quarter:] = (total[:, quarter:] + more).astype(BF16)


def weight_gradient(scale, cot_own, hid_own, g1, g2, g3, n2, f1, f2, f3, pieces, to_bwd, cot, hid, hid_t):
    rows, half = cot_own.shape[0], cot_own.shape[1] // 2
    store_swapped(lax.axis_index("core"), cot.at[:rows], cot_own[...])
    hid_t[:, :rows] = hid_own[...]
    for k, (got, near, far) in enumerate(((g1, g1, f1), (g2, n2, f2), (g3, g3, f3))):
        here = slice((k + 1) * rows, (k + 2) * rows)
        cot[here, :half] = near[:, :half]
        cot[here, half:] = far[...]
        for i in range(NZ * SLOT // rows):
            from_column = got.shape[1] - NZ * SLOT + i * rows
            hid_t[i * rows : (i + 1) * rows, here] = got[:, from_column : from_column + rows]
    z = lax.axis_index("z")

    @pl.loop(0, cot.shape[1] // TILE)
    def _(t):
        columns = pl.ds(pl.multiple_of(t * TILE, TILE), TILE)
        product = jnp.dot(hid_t[...], cot[:, columns], preferred_element_type=F32) * scale
        for block in range(NZ):
            distance = lax.rem(block - z + NZ, NZ)
            pieces[distance, :, columns] = product[block * SLOT : block * SLOT + SENT]

    to_bwd[...] = pieces[NZ // 2].astype(BF16)
    hid[...] = hid_t[...].T


def padded(piece):
    rows, width = piece.shape
    return jnp.concatenate([piece[...].astype(F32), jnp.zeros((SLOT - rows, width), F32)], 0).astype(BF16)


def near_blocks(w0, f1, f2, f3, b3, b2, b1, hid, weight, product, opposite, other, mark):
    z = lax.axis_index("z")
    width = w0.shape[1]
    half = width // 2
    for distance, piece in enumerate((w0, f1, f2, f3, None, b3, b2, b1)):
        to = lax.rem(z - distance + NZ, NZ)
        if piece is None:
            weight[to] = jnp.zeros((SLOT, width), BF16)
        else:
            weight[to] = padded(piece)

    @pl.loop(0, half // TILE)
    def _(t):
        here = pl.ds(pl.multiple_of(t * TILE, TILE), TILE)
        there = pl.ds(pl.multiple_of(half + t * TILE, TILE), TILE)
        rhs = weight[:, :, there].reshape(NZ * SLOT, TILE)
        other[:, here] = jnp.dot(hid[...], rhs, preferred_element_type=F32).astype(BF16)
        rhs = weight[:, :, here].reshape(NZ * SLOT, TILE)
        product[:, here] = jnp.dot(hid[...], rhs, preferred_element_type=F32)

    for block in range(NZ):

        @pl.when(z == (block + NZ // 2) % NZ)
        def _(block=block):
            some = hid[:, block * SLOT : (block + 1) * SLOT]
            opposite[...] = some
            other[:, half:] = jnp.concatenate([some, jnp.zeros_like(some)], 1)

    mark[...] = w0[: mark.shape[0], : mark.shape[1]]


def other_half(block, mark, out):
    out[...] = block[:, out.shape[1] :]


def output_parts(product, crossed, opposite, block, block_other, total, m1, m3, keep, give, second):
    rows, half = total.shape
    quarter = half // 2
    own, far = padded(block.at[:, :half]), padded(block_other)
    far_hidden = crossed[:, half : half + SLOT]
    for t in range(half // TILE):
        here = slice(t * TILE, (t + 1) * TILE)
        value = product[:, here] + crossed[:, here].astype(F32)
        value = value + jnp.dot(opposite[...], own[:, here], preferred_element_type=F32)
        value = value + jnp.dot(far_hidden, far[:, here], preferred_element_type=F32)
        total[:, here] = value[:rows]
        m1[:, here] = value[rows : 2 * rows].astype(BF16)
        second[:, here] = value[2 * rows : 3 * rows]
        m3[:, here] = value[3 * rows : 4 * rows].astype(BF16)

    @pl.when(lax.axis_index("yl") == 0)
    def _():
        keep[...] = second[:, :quarter]
        give[...] = second[:, quarter:].astype(BF16)

    @pl.when(lax.axis_index("yl") != 0)
    def _():
        keep[...] = second[:, quarter:]
        give[...] = second[:, :quarter].astype(BF16)


def first_rows(value, out):
    out[...] = value[: out.shape[0], : out.shape[1]]


def add_given(keep, given, out):
    out[...] = (keep[...] + given[...].astype(F32)).astype(BF16)


def back_parts(cot, weight, block, *parts):
    slots = TILE // SLOT
    rows = parts[0].shape[1]
    dims = (((1,), (1,)), ((), ()))

    @pl.loop(0, NZ // slots)
    def _(t):
        some = weight[pl.ds(t * slots, slots)].reshape(TILE, weight.shape[2])
        product = lax.dot_general(some, cot[...], dims, preferred_element_type=F32)
        for k, part in enumerate(parts):
            part[pl.ds(pl.multiple_of(t * TILE, TILE), TILE)] = product[
                :, k * rows : (k + 1) * rows
            ].astype(BF16)

    opposite = lax.rem(lax.axis_index("z") + NZ // 2, NZ)
    product = lax.dot_general(padded(block), cot[...], dims, preferred_element_type=F32)
    for k, part in enumerate(parts):
        part[pl.ds(pl.multiple_of(opposite * SLOT, SLOT), SLOT)] = product[
            :, k * rows : (k + 1) * rows
        ].astype(BF16)


def activation_factors(gate, up, of_gate, of_up):
    gate32, up32 = gate[...].astype(F32), up[...].astype(F32)
    sig = jax.nn.sigmoid(gate32)
    of_gate[...] = up32 * (sig * (1.0 + gate32 * (1.0 - sig)))
    of_up[...] = gate32 * sig


def activation_gradients(of_gate, of_up, b0, b1, b2, b3, grad_gate, grad_up, back32):
    units, rows = of_gate.shape
    used = units // (NX * NZ)
    for x in range(NX):

        @pl.when(lax.axis_index("x") == x)
        def _(x=x):
            for s in range(NX):
                source = (b0, b1, b2, b3)[(s - x) % NX]
                for block in range(NZ):
                    value = source[block * SLOT : (block + 1) * SLOT].astype(F32)
                    start = (s * NZ + block) * used
                    back32[start : start + used] = value[:used]

    grad_gate[...] = (back32[...] * of_gate[...]).astype(BF16)
    grad_up[...] = (back32[...] * of_up[...]).astype(BF16)


def add_pieces(distance, others, pieces, *refs):
    *sums, to_fwd, to_bwd = refs[others:]
    here = pieces[distance]
    if len(sums) > 1:
        here = here + sums[0][...].astype(F32)
    to_fwd[...] = here.astype(BF16)
    to_bwd[...] = (pieces[NZ - distance] + sums[-1][...].astype(F32)).astype(BF16)


def finish_rows(pieces, fwd, bwd, keep, give, total):
    rows, half = keep.shape[0], keep.shape[1] // 2
    core, yh = lax.axis_index("core"), lax.axis_index("yh")
    store_swapped(core, total, pieces[0] + (fwd[...].astype(F32) + bwd[...].astype(F32)))

    @pl.when(yh == 0)
    def _():
        keep[...] = total[:rows]
        give[...] = total[rows : 2 * rows].astype(BF16)

    @pl.when(yh != 0)
    def _():
        keep[...] = total[rows : 2 * rows]
        give[...] = total[:rows].astype(BF16)


def finish(mine, other, keep, taken, out, grad):
    half = mine.shape[1]

    @pl.when(lax.axis_index("core") == 0)
    def _():
        out[:, :half] = mine[...]
        out[:, half:] = other[...]

    @pl.when(lax.axis_index("core") != 0)
    def _():
        out[:, :half] = other[...]
        out[:, half:] = mine[...]

    grad[...] = keep[...] + taken[...].astype(F32)


def body(gate_pre, up_pre, down_weight, cotangent):
    gate, up = gate_pre.T, up_pre.T
    units, rows = gate.shape
    block, width = down_weight.shape
    half = width // 2
    slots = NZ * SLOT
    tokens = NX * rows
    wide = half + slots

    w_other = shift(down_weight, "yh", 1)
    m1, m2, m3, hid_own = call(
        prepare,
        [like((rows, wide)), like((rows, wide - half // 2)), like((rows, wide))]
        + [like((slots, rows))],
        gate, up, cotangent,
        scratch=[pltpu.VMEM((rows, width), BF16)]
        + [pltpu.VMEM((units, rows), BF16)] * 2
        + [pltpu.VMEM((units + SLOT, rows), F32), pltpu.VMEM((NX, rows, slots), BF16)]
        + [pltpu.SemaphoreType.DMA((3 * NX + 6 + slots // rows,))],
        out_space=pltpu.HBM,
        space=pltpu.HBM,
        limit=56,
    )
    w_other = after(w_other, m1, m2, m3)
    (w0,) = call(pack_weight, [like((SENT, width))], down_weight, w_other, flops=18 * 10**8)
    got = [shift(m, "x", k) for k, m in ((1, m1), (2, m2), (3, m3))]

    nears = call(
        near_halves,
        [like((rows, half))] * 3,
        *got, shift(got[1], "yl", 1),
        flops=200 * 10**6,
        moved=0,
    )
    far = [shift(near, "core", 1) for near in nears]

    fwd, bwd = [w0], [w0]
    for step in range(3):
        f, b = shift(fwd[-1], "z", 1), shift(bwd[-1], "z", -1)
        f, b = lax.optimization_barrier((f, b))
        fwd.append(f)
        bwd.append(b)
    scale = float(tokens * NZ * 2) ** (-0.5)
    pieces, to_bwd, cot, hid = call(
        functools.partial(weight_gradient, scale),
        [like((NZ, SENT, width), F32), like((SENT, width)), like((tokens, width)), like((tokens, slots))],
        cotangent, hid_own, *got, nears[1], *far,
        scratch=[pltpu.VMEM((slots, tokens), BF16)],
        flops=0,
        moved=0,
    )

    def added(distance, ring, *others):
        kernel = functools.partial(add_pieces, distance, len(others))
        return call(kernel, [like((SENT, width))] * 2, pieces, *others, *ring, moved=0)

    f4 = shift(fwd[3], "z", 1)
    ring = (shift(to_bwd, "z", -1),)

    weight, product, opposite, other, early = call(
        near_blocks,
        [like((NZ, SLOT, width)), like((tokens, half), F32), like((tokens, SLOT))]
        + [like((tokens, half + 2 * SLOT)), like((16, 128))],
        *fwd, *reversed(bwd[1:]), hid,
        moved=0,
    )
    crossed = shift(other, "core", 1)
    to_fwd, to_bwd = added(3, ring, early)
    ring = (shift(to_fwd, "z", 1), shift(to_bwd, "z", -1))

    (mark,) = call(first_rows, [like((16, 128))], to_fwd, flops=2 * 10**9)
    (block_half,) = call(other_half, [like((SENT, half))], f4, mark, flops=14 * 10**9)
    total, m1, m3, keep2, give2 = call(
        output_parts,
        [like((rows, half), F32)] + [like((rows, half))] * 2
        + [like((rows, half // 2), F32), like((rows, half // 2))],
        product, crossed, opposite, f4, shift(block_half, "core", 1),
        scratch=[pltpu.VMEM((rows, half), F32)],
        flops=1 * 10**9,
        moved=0,
    )
    given2 = shift(give2, "yl", 1)
    got1, got3 = shift(m1, "x", -1), shift(m3, "x", -3)
    (m2,) = call(add_given, [like((rows, half // 2))], keep2, given2, moved=0)
    got_out = [got1, shift(m2, "x", -2), got3]
    back_own, *backs = call(
        back_parts, [like((slots, rows))] * NX, after(cot, m1), weight, f4, moved=0
    )
    back1, back2, back3 = backs
    ring = after(ring, m1, m3)
    to_fwd, to_bwd = added(2, ring)
    ring = (shift(to_fwd, "z", 1), shift(to_bwd, "z", -1))
    of_gate, of_up = call(activation_factors, [like((units, rows), F32)] * 2, gate, up, moved=0)
    *ring, back1, back2, back3, of_gate, of_up = lax.optimization_barrier(
        (*ring, back1, back2, back3, of_gate, of_up)
    )
    got_back1, got_back2 = shift(back1, "x", -1), shift(back2, "x", -2)
    to_fwd, to_bwd = added(1, ring)
    got_out = after(got_out, to_fwd, to_bwd)
    ring = (shift(to_fwd, "z", 1), shift(to_bwd, "z", -1))
    (rounded,) = call(add_up, [like((rows, half))], total, *got_out, moved=0)
    across = shift(rounded, "yl", 1)
    ring = after(ring, rounded)
    keep, give = call(
        finish_rows,
        [like((block, width), F32), like((block, width))],
        pieces, *ring,
        scratch=[pltpu.VMEM((SENT, width), F32)],
        flops=60 * 10**7,
        moved=0,
    )
    taken = shift(give, "yh", 1)
    got_back3 = shift(after(back3, give), "x", -3)
    grad_gate, grad_up = call(
        activation_gradients,
        [like((units, rows))] * 2,
        of_gate, of_up, back_own, got_back1, got_back2, got_back3,
        scratch=[pltpu.VMEM((units, rows), F32)],
        flops=400 * 10**7,
        moved=0,
    )
    across = after(across, give)
    out_half = (rounded.astype(F32) + across.astype(F32)).astype(BF16)
    output, grad_weight = call(
        finish,
        [like((rows, width)), like((block, width), F32)],
        out_half, shift(out_half, "core", 1), keep, taken,
    )
    return output, grad_weight, grad_gate.T, grad_up.T


def solution(mesh):
    fine = Mesh(mesh.devices.reshape(2, 2, NX, NZ, 2), ("yl", "core", "x", "z", "yh"))
    blk, dp = ("x", "z", "yh"), ("yl", "core")
    return jax.shard_map(
        body,
        mesh=fine,
        in_specs=(P(blk, dp), P(blk, dp), P(dp + blk, None), P(blk, None)),
        out_specs=(P(blk, None), P(dp + blk, None), P(blk, dp), P(blk, dp)),
        check_vma=False,
    )
```
